32 devices in a mesh: dp: 4 (over y, x), key: 8 (over z, core).
Axes of the slice: x: 2, y: 2, z: 4, core: 2. Of those that a mesh axis runs over, the one named last changes fastest.
Arguments:
- inputs: bfloat16 [32, 512, 1024], P(('dp', 'key')), may hold values from -6 to 6
- positions: int32 [32, 512], P(('dp', 'key')), may hold values from 0 to 2045, as said below
- memory_flag: int32 [32], P('dp'), may hold values from 0 to 1, as said below
- partner: int32 [32], P('dp'), may hold values from 0 to 7, as said below
- cache_keys: bfloat16 [32, 512, 1024], P('dp', 'key'), may hold values from -6 to 6
- cache_values: bfloat16 [32, 512, 1024], P('dp', 'key'), may hold values from -6 to 6
- query_proj: bfloat16 [1024, 1024], P('key'), may hold values from -0.1875 to 0.1875
- key_proj: bfloat16 [1024, 1024], P('key'), may hold values from -0.1875 to 0.1875
- value_proj: bfloat16 [1024, 1024], P('key'), may hold values from -0.1875 to 0.1875
- out_proj: bfloat16 [1024, 1024], P('key'), may hold values from -3 to 3
- gate_proj: bfloat16 [1024, 2816], P('key'), may hold values from -0.1875 to 0.1875
- up_proj: bfloat16 [1024, 2816], P('key'), may hold values from -0.1875 to 0.1875
- down_proj: bfloat16 [2816, 1024], P('key'), may hold values from -0.109375 to 0.109375
- attn_gain: bfloat16 [1024], P('key'), may hold values from 0.099609375 to 1.8984375
- ffn_gain: bfloat16 [1024], P('key'), may hold values from 0.099609375 to 1.8984375
- cotangent: bfloat16 [32, 512, 1024], P(('dp', 'key')), may hold values from -6 to 6
Outputs:
- outputs: bfloat16 [32, 512, 1024], P(('dp', 'key'))
- input_grad: float32 [32, 512, 1024], P(('dp', 'key'))
- grad_query: float32 [1024, 1024], P('key')
- grad_key: float32 [1024, 1024], P('key')
- grad_value: float32 [1024, 1024], P('key')
- grad_out: float32 [1024, 1024], P('key')
- grad_gate: float32 [1024, 2816], P('key')
- grad_up: float32 [1024, 2816], P('key')
- grad_down: float32 [2816, 1024], P('key')
- grad_attn_gain: float32 [1024], P('key')
- grad_ffn_gain: float32 [1024], P('key')
- new_keys: bfloat16 [32, 512, 1024], P('dp', 'key')
- new_values: bfloat16 [32, 512, 1024], P('dp', 'key')
The draws below stay inside these ranges and needn't reach their ends.
Inputs may be any that keep to these rules, and one draw needn't show every extreme that they name: `positions`: within a segment a token's position is one more than the token before it, except at exactly one document start (never the segment's first token) where it is 0. `memory_flag`: exactly half of each group of 8 consecutive segments has 1. Names another segment of the same group of 8 consecutive segments by its index within the group, never the segment itself; each segment of a group is the partner of exactly one segment.
All inputs are finite; a program needn't handle non-finite values.
Results may differ from the reference program's by a relative error of at most 0.017.
Values may be sent and summed in bfloat16 or wider, within the bound.
No kernel may reach another device: no remote copies, remote signals or barrier semaphores. Data moves between devices by JAX's collectives and lax.ppermute only.
A program may use at most 256 MiB of HBM per device.

```python
import math
from functools import partial
import jax
import jax.numpy as jnp
from jax import lax

D = 1024
H = 8
HD = 128
FF = 2816
SEG = 512
MEMORY = 512
SEGMENTS = 32
N_KEY = 8


def group_orders(key):
    group_count = SEGMENTS // N_KEY
    raw_scores = jax.random.randint(key, (group_count, N_KEY), 0, 1 << 20)
    distinct = raw_scores * N_KEY + jnp.arange(N_KEY, dtype=jnp.int32)[None, :]
    return jnp.argsort(distinct, axis=1).astype(jnp.int32)


def draw_positions(key, part):
    key = jax.random.fold_in(key, 11)
    first_key, second_key = jax.random.split(key)
    token_order = jnp.arange(SEG, dtype=jnp.int32)
    segment_order = jnp.arange(SEGMENTS, dtype=jnp.int32)[:, None]
    start_at = jax.random.randint(first_key, (SEGMENTS, 1), 1, SEG)
    offset = jax.random.randint(second_key, (SEGMENTS, 1), 0, 3 * SEG)
    start_at = jnp.where(segment_order == 0, SEG - 1, start_at)
    offset = jnp.where(segment_order == 0, 3 * SEG - 1, offset)
    last_start = jnp.where(token_order[None, :] >= start_at, start_at, -offset)
    return (token_order[None, :] - last_start).astype(jnp.int32)


def draw_memory_flag(key, part):
    key = jax.random.fold_in(key, 12)
    permuted = group_orders(key)
    rank_of = jnp.argsort(permuted, axis=1)
    return (rank_of < N_KEY // 2).astype(jnp.int32).reshape(-1)


def draw_partner(key, part):
    key = jax.random.fold_in(key, 13)
    permuted = group_orders(key)
    rank_of = jnp.argsort(permuted, axis=1)
    following = jnp.take_along_axis(permuted, (rank_of + 1) % N_KEY, axis=1)
    return following.astype(jnp.int32).reshape(-1)


def block_levels(key, shape, pieces, smallest, high):
    factor_of, own = 1.0, jax.random.fold_in(key, 6)
    for dim, parts in pieces:
        heights = jnp.exp(jax.random.uniform(jax.random.fold_in(own, dim), (parts,), jnp.float32, smallest / len(pieces), high / len(pieces)))
        factor_of = factor_of * jnp.repeat(heights, shape[dim] // parts).reshape([-1 if axis == dim else 1 for axis in range(len(shape))])
    return factor_of


def bell_draw(key, shape, scale, reach, cuts=(), kind=jnp.bfloat16):
    drawn = scale * jax.random.normal(key, shape, jnp.float32)
    if cuts:
        drawn = drawn * block_levels(key, shape, cuts, -0.22, 0.18)
    return jnp.clip(drawn, -reach, reach).astype(kind)


def setup_inputs(seed: int = 0) -> dict:
    splits = jax.random.split(jax.random.key(seed), 17)
    return {
        "inputs": bell_draw(splits[0], (SEGMENTS, SEG, D), 1.0, 6.0, ((0, 32),)),
        "positions": draw_positions(jax.random.fold_in(splits[16], 71), 0),
        "memory_flag": draw_memory_flag(jax.random.fold_in(splits[16], 71), 0),
        "partner": draw_partner(jax.random.fold_in(splits[16], 71), 0),
        "cache_keys": bell_draw(splits[4], (SEGMENTS, MEMORY, D), 1.0, 6.0, ((0, 4), (1, 8))),
        "cache_values": bell_draw(splits[5], (SEGMENTS, MEMORY, D), 1.0, 6.0, ((0, 4), (1, 8))),
        "query_proj": bell_draw(splits[6], (D, D), D ** -0.5, 0.1875, ((0, 8),)),
        "key_proj": bell_draw(splits[7], (D, D), D ** -0.5, 0.1875, ((0, 8),)),
        "value_proj": bell_draw(splits[8], (D, D), D ** -0.5, 0.1875, ((0, 8),)),
        "out_proj": bell_draw(splits[9], (D, D), (max(D // 256, 1)) ** -0.5, 3.0, ((0, 8),)),
        "gate_proj": bell_draw(splits[10], (D, FF), D ** -0.5, 0.1875, ((0, 8),)),
        "up_proj": bell_draw(splits[11], (D, FF), D ** -0.5, 0.1875, ((0, 8),)),
        "down_proj": bell_draw(splits[12], (FF, D), FF ** -0.5, 0.109375, ((0, 8),)),
        "attn_gain": jnp.clip(1.0 + 0.18 * jax.random.normal(splits[13], (D,), jnp.float32), 0.099609375, 1.8984375).astype(jnp.bfloat16),
        "ffn_gain": jnp.clip(1.0 + 0.18 * jax.random.normal(splits[14], (D,), jnp.float32), 0.099609375, 1.8984375).astype(jnp.bfloat16),
        "cotangent": bell_draw(splits[15], (SEGMENTS, SEG, D), 1.0, 6.0, ((0, 32),)),
    }


@jax.custom_vjp
def low(v):
    return lax.optimization_barrier(v.astype(jnp.bfloat16)).astype(jnp.float32)

@jax.custom_vjp
def low_back(v):
    return v

def low_keep(v):
    return (low(v), None)

def low_pass(kept, grad):
    return (grad,)

def back_keep(v):
    return (v, None)

def back_low(kept, grad):
    return (low(grad),)
low.defvjp(low_keep, low_pass)
low_back.defvjp(back_keep, back_low)
EPSILON = 1e-05
ROPE_BASE = 10000.0
NEG_FILL = -1e+30

def highest(left, right):
    return jnp.dot(left, right, precision=lax.Precision.HIGHEST)

def rms_normed(values, gain_values):
    inverse_rms = lax.rsqrt(lax.optimization_barrier(jnp.mean(values * values, axis=-1, keepdims=True)) + EPSILON)
    return values * inverse_rms * gain_values

def rotary_tables(token_positions, head_width):
    half_width = head_width // 2
    frequency = ROPE_BASE ** (-2.0 * jnp.arange(half_width, dtype=jnp.float32) / head_width)
    angles = token_positions.astype(jnp.float32)[:, None] * frequency[None, :]
    return (jnp.cos(angles), jnp.sin(angles))

def rotate(values, cosine, sine_table):
    row_count = values.shape[0]
    split_heads = values.reshape(row_count, H, HD)
    half_width = HD // 2
    first_half = split_heads[:, :, :half_width]
    second = split_heads[:, :, half_width:]
    cos_rows = cosine[:, None, :]
    sin_rows = sine_table[:, None, :]
    turned = jnp.concatenate([first_half * cos_rows - second * sin_rows, second * cos_rows + first_half * sin_rows], axis=-1)
    return turned.reshape(row_count, H * HD)

def segment_forward(segment_inputs, segment_positions, flag_value, own_keys, own_values, partner_keys, partner_values, weight_list):
    query_proj, key_proj, value_proj, out_proj, gate_proj, up_proj, down_proj, attn_gain, ffn_gain = weight_list
    token_count = segment_inputs.shape[0]
    normed_attn = low(rms_normed(segment_inputs, attn_gain))
    query_raw = low_back(highest(normed_attn, query_proj))
    key_raw = low_back(highest(normed_attn, key_proj))
    value_raw = low_back(highest(normed_attn, value_proj))
    cosine, sine_table = rotary_tables(segment_positions, HD)
    query_mem = low(query_raw)
    query_loc = low(rotate(query_raw, cosine, sine_table))
    key_loc = low(rotate(key_raw, cosine, sine_table))
    value_loc = low(value_raw)
    memory_keys = jnp.concatenate([own_keys, partner_keys], axis=0)
    memory_values = jnp.concatenate([own_values, partner_values], axis=0)
    scale_factor = 1.0 / math.sqrt(HD)
    local_part = jnp.einsum('qhd,khd->hqk', query_loc.reshape(token_count, H, HD), key_loc.reshape(token_count, H, HD), precision=lax.Precision.HIGHEST)
    memory_part = jnp.einsum('qhd,khd->hqk', query_mem.reshape(token_count, H, HD), memory_keys.reshape(-1, H, HD), precision=lax.Precision.HIGHEST)
    scores = low_back(jnp.concatenate([local_part, memory_part], axis=-1) * scale_factor)
    token_order = jnp.arange(token_count, dtype=jnp.int32)
    local_valid = (token_order[None, :] <= token_order[:, None]) & (segment_positions[:, None] - segment_positions[None, :] == token_order[:, None] - token_order[None, :])
    memory_valid = (jnp.arange(2 * MEMORY, dtype=jnp.int32) >= MEMORY) | (flag_value == 1)
    key_valid = jnp.concatenate([local_valid, jnp.broadcast_to(memory_valid[None, :], (token_count, 2 * MEMORY))], axis=-1)
    masked = jnp.where(key_valid[None], scores, NEG_FILL)
    largest = lax.optimization_barrier(jnp.max(masked, axis=-1, keepdims=True))
    shifted = jnp.exp(masked - largest)
    softmax_probs = shifted / lax.optimization_barrier(jnp.sum(shifted, axis=-1, keepdims=True))
    probs_low = low(softmax_probs)
    value_heads = jnp.concatenate([value_loc, memory_values], axis=0).reshape(-1, H, HD)
    attended = jnp.einsum('hqk,khd->qhd', probs_low, value_heads, precision=lax.Precision.HIGHEST).reshape(token_count, D)
    attended = low(low_back(attended))
    branch = low_back(highest(attended, out_proj))
    mixed_rows = segment_inputs + branch
    normed_ff = low(rms_normed(mixed_rows, ffn_gain))
    gate_raw = low_back(highest(normed_ff, gate_proj))
    up_raw = low_back(highest(normed_ff, up_proj))
    hidden = low(jax.nn.silu(gate_raw) * up_raw)
    outputs = mixed_rows + highest(hidden, down_proj)
    return (outputs, low(key_raw), value_loc)

def refresh(cache_array, fresh_array, seg_total):
    slot_count = MEMORY // N_KEY
    new_count = SEG // N_KEY
    old_blocks = cache_array.reshape(seg_total, N_KEY, slot_count, D)
    incoming = fresh_array.reshape(seg_total, N_KEY, new_count, D)
    merged = jnp.concatenate([old_blocks[:, :, new_count:], incoming], axis=2)
    return merged.reshape(seg_total, MEMORY, D)

def reference(inputs, positions, memory_flag, partner, cache_keys, cache_values, query_proj, key_proj, value_proj, out_proj, gate_proj, up_proj, down_proj, attn_gain, ffn_gain, cotangent):
    seg_total = inputs.shape[0]
    group_size = math.gcd(seg_total, max(1, 2048 // SEG))
    group_total = seg_total // group_size
    seg_order = jnp.arange(seg_total, dtype=jnp.int32)
    partner_global = seg_order // N_KEY * N_KEY + partner.astype(jnp.int32)
    weight_inputs = tuple((weight_item.astype(jnp.float32) for weight_item in (query_proj, key_proj, value_proj, out_proj, gate_proj, up_proj, down_proj, attn_gain, ffn_gain)))

    def grouped(array_in):
        return array_in.reshape((group_total, group_size) + array_in.shape[1:])

    def forward(inputs_all, *weight_list):

        def one_group(items):
            block_inputs, block_positions, block_flags, block_own, block_partner = items
            own_keys = jnp.take(cache_keys, block_own, axis=0).astype(jnp.float32)
            own_values = jnp.take(cache_values, block_own, axis=0).astype(jnp.float32)
            partner_keys = jnp.take(cache_keys, block_partner, axis=0).astype(jnp.float32)
            partner_values = jnp.take(cache_values, block_partner, axis=0).astype(jnp.float32)
            mapped = jax.vmap(partial(segment_forward, weight_list=weight_list))
            return mapped(block_inputs, block_positions, block_flags, own_keys, own_values, partner_keys, partner_values)
        results = lax.map(jax.checkpoint(one_group), (inputs_all, grouped(positions), grouped(memory_flag), grouped(seg_order), grouped(partner_global)))
        return (results[0], (results[1], results[2]))
    outputs, pull_back, fresh = jax.vjp(forward, grouped(inputs.astype(jnp.float32)), *weight_inputs, has_aux=True)
    gradients = pull_back(grouped(cotangent.astype(jnp.float32)))
    fresh_keys = fresh[0].reshape(seg_total, SEG, D).astype(jnp.bfloat16)
    fresh_values = fresh[1].reshape(seg_total, SEG, D).astype(jnp.bfloat16)
    new_keys = refresh(cache_keys, fresh_keys, seg_total)
    new_values = refresh(cache_values, fresh_values, seg_total)
    return (outputs.reshape(seg_total, SEG, D).astype(jnp.bfloat16), gradients[0].reshape(seg_total, SEG, D), gradients[1], gradients[2], gradients[3], gradients[4], gradients[5], gradients[6], gradients[7], gradients[8], gradients[9], new_keys, new_values)
```

```python
import functools
import math

import jax
import jax.numpy as jnp
from jax import lax
from jax.experimental import pallas as pl
from jax.experimental.pallas import tpu as pltpu
from jax.sharding import PartitionSpec as P

H = 8
HD = 128
EPSILON = 1e-05
ROPE_BASE = 10000.0
NEG_FILL = -1e30
SCALE = 1.0 / math.sqrt(HD)
BF16 = jnp.bfloat16
F32 = jnp.float32
COLS = 256
GAIN_ROWS = 16
VMEM_LIMIT = 58 * 1024 * 1024


def dot(left, right):
    return jnp.dot(left, right, preferred_element_type=F32)


def dot_nt(left, right):
    return lax.dot_general(left, right, (((1,), (1,)), ((), ())), preferred_element_type=F32)


def dot_tn(left, right):
    return lax.dot_general(left, right, (((0,), (0,)), ((), ())), preferred_element_type=F32)


def inverse_rms(values):
    return lax.rsqrt(jnp.mean(values * values, axis=-1, keepdims=True) + EPSILON)


def turn(values, cosine, sine):
    return values * cosine + pltpu.roll(values, HD // 2, 1) * sine


class Plan:
    def __init__(self, n_dp, n_key):
        self.n_dp, self.n_key = n_dp, n_key
        self.fast = n_dp == 4 and n_key == 8
        self.halves = 2 if self.fast else 1


def swap(values, axis, size, distance):
    return lax.ppermute(values, axis, [(i, i ^ distance) for i in range(size)])


def own_quarter(weight, n_dp):
    width = weight.shape[1] // n_dp
    return lax.dynamic_slice_in_dim(weight, lax.axis_index("dp") * width, width, 1)


def along_z(quarter):
    return jnp.stack([quarter] + [swap(quarter, "key", 8, 2 * r) for r in (1, 2, 3)])


def across(held):
    return [held] + [swap(held, "dp", 4, r) for r in (1, 2, 3)]


def other_core(pieces):
    return [swap(piece, "key", 8, 1) for piece in pieces]


def after(values, token):
    return lax.optimization_barrier((values, token))[0]


def place(plan, pieces, first_row, rows, target, sem):
    copies = []
    q, key = lax.axis_index("dp"), lax.axis_index("key")
    for core in range(2):
        for far in range(4):
            for zr in range(4):
                block = key ^ (2 * zr + core)
                row = pl.multiple_of(block * rows, 16)
                column = pl.multiple_of((q ^ far) * COLS, COLS)
                copies.append(
                    pltpu.make_async_copy(
                        pieces[core * 4 + far].at[zr, pl.ds(first_row, rows)],
                        target.at[pl.ds(row, rows), pl.ds(column, COLS)],
                        sem,
                    )
                )
    return copies


def row_blocks(plan, width):
    if not plan.fast:
        return [(0, None, None, width)]
    rows = width // (plan.n_key * plan.n_dp)
    return [((z * 2 + c) * 4 + q, (z, c, q), None, rows) for z in range(4) for c in range(2) for q in range(4)]


def store_turned(plan, values, target, relative):
    turned = values.T
    if not plan.fast:
        target[0] = turned
        return
    q, key = lax.axis_index("dp"), lax.axis_index("key")
    core, z = lax.rem(key, 2), key // 2
    for natural, (zz, cc, qq), _, rows in row_blocks(plan, turned.shape[0]):
        qi = (q ^ qq) if relative else qq
        zi = (z ^ zz) if relative else zz
        row = pl.multiple_of((qi * 4 + zi) * rows, rows)
        target[core ^ cc, pl.ds(row, rows), :] = turned[natural * rows : (natural + 1) * rows]


def project_kernel(plan, n_pieces, x_ref, cos_ref, sin_ref, *refs):
    pieces, refs = refs[:n_pieces], refs[n_pieces:]
    qmem_ref, qloc_ref, kloc_ref, kraw_ref, v_ref, normed_ref, gains_ref, w_ref, g_ref, sems = refs
    width = x_ref.shape[1]
    if plan.fast:
        rows = width // plan.n_key
        copies = []
        for m in range(3):
            copies += place(plan, pieces, GAIN_ROWS + m * rows, rows, w_ref.at[m], sems.at[0])
        key = lax.axis_index("key")
        for core in range(2):
            for zr in range(4):
                copies.append(
                    pltpu.make_async_copy(
                        pieces[core * 4].at[zr, pl.ds(0, GAIN_ROWS)],
                        g_ref.at[key ^ (2 * zr + core)],
                        sems.at[1],
                    )
                )
        for copy in copies:
            copy.start()
        pltpu.make_async_copy(g_ref, g_ref, sems.at[1]).wait()
        lead = [g_ref[k][0:1, :].astype(F32) for k in range(plan.n_key)]
        attn_gain = jnp.concatenate([row[:, :rows] for row in lead], axis=1)
        ffn_gain = jnp.concatenate([row[:, rows:] for row in lead], axis=1)
    else:
        copy = pltpu.make_async_copy(pieces[0], w_ref, sems.at[0])
        copy.start()
        attn_gain = pieces[1][0:1, :]
        ffn_gain = pieces[1][1:2, :]
    gains_ref[0:1, :] = attn_gain
    gains_ref[1:2, :] = ffn_gain
    x = x_ref[...].astype(F32)
    normed = (x * inverse_rms(x) * attn_gain).astype(BF16)
    normed_ref[...] = normed
    pltpu.make_async_copy(w_ref, w_ref, sems.at[0]).wait()
    cosine, sine = cos_ref[...], sin_ref[...]
    for m in range(3):
        for c in range(width // COLS):
            cols = slice(c * COLS, (c + 1) * COLS)
            raw = dot(normed, w_ref[m, :, cols])
            low = raw.astype(BF16)
            if m == 2:
                v_ref[:, cols] = low
                continue
            (qmem_ref if m == 0 else kraw_ref)[:, cols] = low
            out = qloc_ref if m == 0 else kloc_ref
            for h in range(COLS // HD):
                part = raw[:, h * HD : (h + 1) * HD]
                start = c * COLS + h * HD
                out[:, start : start + HD] = turn(part, cosine, sine).astype(BF16)


def project(plan, x, cosine, sine, pieces):
    tokens, width = x.shape
    whole = pl.BlockSpec(memory_space=pltpu.VMEM)
    anywhere = pl.BlockSpec(memory_space=pl.ANY)
    row = jax.ShapeDtypeStruct((tokens, width), BF16)
    return pl.pallas_call(
        functools.partial(project_kernel, plan, len(pieces)),
        out_shape=[row] * 6 + [jax.ShapeDtypeStruct((2, width), F32)],
        in_specs=[whole] * 3 + ([anywhere] * len(pieces) if plan.fast else [anywhere, whole]),
        out_specs=[whole] * 7,
        scratch_shapes=[
            pltpu.VMEM((3, width, width), BF16),
            pltpu.VMEM((plan.n_key, GAIN_ROWS, COLS), BF16),
            pltpu.SemaphoreType.DMA((2,)),
        ],
        compiler_params=pltpu.CompilerParams(vmem_limit_bytes=VMEM_LIMIT),
        cost_estimate=pl.CostEstimate(
            flops=6 * tokens * width * width, bytes_accessed=16 * 2**20, transcendentals=0
        ),
        name="project",
    )(x, cosine, sine, *pieces)


def memory_of(memory_ref):
    block = memory_ref[...]
    sources, rows, width = block.shape
    half = rows // 2
    keys = block[:, :half].reshape(sources * half, width)
    values = block[:, half:].reshape(sources * half, width)
    return keys, values


def attend_kernel(qmem, qloc, kloc, v, memory, local_bias, memory_bias, out, p_loc, p_mem):
    mem_k, mem_v = memory_of(memory)
    s_loc = dot_nt(qloc[...], kloc[...]) * SCALE + local_bias[...]
    s_mem = dot_nt(qmem[...], mem_k) * SCALE + memory_bias[...]
    largest = jnp.maximum(
        jnp.max(s_loc, axis=-1, keepdims=True), jnp.max(s_mem, axis=-1, keepdims=True)
    )
    e_loc = jnp.exp(s_loc - largest)
    e_mem = jnp.exp(s_mem - largest)
    total = jnp.sum(e_loc, axis=-1, keepdims=True) + jnp.sum(e_mem, axis=-1, keepdims=True)
    inverse = 1.0 / total
    low_loc = (e_loc * inverse).astype(BF16)
    low_mem = (e_mem * inverse).astype(BF16)
    p_loc[0] = low_loc
    p_mem[0] = low_mem
    out[...] = (dot(low_loc, v[...]) + dot(low_mem, mem_v)).astype(BF16)


def attend(qmem, qloc, kloc, v, memory, local_bias, memory_bias):
    tokens, width = qmem.shape
    keys = memory_bias.shape[1]
    head = pl.BlockSpec((tokens, HD), lambda h: (0, h))
    return pl.pallas_call(
        attend_kernel,
        grid=(width // HD,),
        in_specs=[head] * 4
        + [
            pl.BlockSpec(memory.shape[:2] + (HD,), lambda h: (0, 0, h)),
            pl.BlockSpec((tokens, tokens), lambda h: (0, 0)),
            pl.BlockSpec((1, keys), lambda h: (0, 0)),
        ],
        out_specs=[
            head,
            pl.BlockSpec((1, tokens, tokens), lambda h: (h, 0, 0)),
            pl.BlockSpec((1, tokens, keys), lambda h: (h, 0, 0)),
        ],
        out_shape=[
            jax.ShapeDtypeStruct((tokens, width), BF16),
            jax.ShapeDtypeStruct((width // HD, tokens, tokens), BF16),
            jax.ShapeDtypeStruct((width // HD, tokens, keys), BF16),
        ],
        compiler_params=pltpu.CompilerParams(vmem_limit_bytes=VMEM_LIMIT),
        cost_estimate=pl.CostEstimate(
            flops=4 * tokens * (tokens + keys) * width,
            bytes_accessed=24 * 2**20,
            transcendentals=tokens * (tokens + keys) * (width // HD),
        ),
        name="attend",
    )(qmem, qloc, kloc, v, memory, local_bias, memory_bias)


def feed_kernel(plan, n_pieces, x_ref, att_ref, ct_ref, gains_ref, gate_ref, up_ref, *refs):
    pieces, refs = refs[:n_pieces], refs[n_pieces:]
    n_half = plan.halves
    gu_refs, refs = refs[:n_half], refs[n_half:]
    (gd_ref, go_ref, out_ref, dmix_ref, datt_ref, dgain_ref) = refs[:6]
    wo, wd, mixed, normed, turned, acc_out, acc_back, sems = refs[6:]
    step = pl.program_id(0)
    width = x_ref.shape[1]
    gain = gains_ref[1:2, :]

    @pl.when(step == 0)
    def _():
        if plan.fast:
            rows = width // plan.n_key
            for copy in place(plan, pieces, 0, rows, wo, sems.at[0]):
                copy.start()
            for copy in place(plan, pieces, rows, wd.shape[0] // plan.n_key, wd, sems.at[1]):
                copy.start()
        else:
            pltpu.make_async_copy(pieces[0], wo, sems.at[0]).start()
            pltpu.make_async_copy(pieces[1], wd, sems.at[1]).start()
        pltpu.make_async_copy(wo, wo, sems.at[0]).wait()
        mixed[...] = x_ref[...].astype(F32) + dot(att_ref[...], wo[...])
        value = mixed[...]
        low = (value * inverse_rms(value) * gain).astype(BF16)
        normed[...] = low
        store_turned(plan, low, turned, False)
        acc_out[...] = jnp.zeros_like(acc_out)
        acc_back[...] = jnp.zeros_like(acc_back)
        pltpu.make_async_copy(wd, wd, sems.at[1]).wait()

    ct = ct_ref[...]
    down = wd[pl.ds(pl.multiple_of(step * COLS, COLS), COLS), :]
    gate = dot(normed[...], gate_ref[...])
    up = dot(normed[...], up_ref[...])
    back = dot_nt(ct, down)
    sigma = 1.0 / (1.0 + jnp.exp(-gate))
    swish = gate * sigma
    hidden = (swish * up).astype(BF16)
    d_gate = (back * up * (sigma * (1.0 + gate * (1.0 - sigma)))).astype(BF16)
    d_up = (back * swish).astype(BF16)
    acc_out[...] += dot(hidden, down)
    acc_back[...] += dot_nt(d_gate, gate_ref[...]) + dot_nt(d_up, up_ref[...])
    grad_down = dot_tn(hidden, ct).astype(BF16)
    for c in range(width // COLS):
        gd_ref[c] = grad_down[:, c * COLS : (c + 1) * COLS]
    for half in range(n_half):
        lead = gu_refs[half].shape[:2]
        for i, grad in enumerate((d_gate, d_up)):
            value = dot(turned[half], grad).astype(BF16)
            gu_refs[half][:, :, i] = value.reshape(lead + (-1, COLS))

    @pl.when(step == pl.num_programs(0) - 1)
    def _():
        value = mixed[...]
        out_ref[...] = (value + acc_out[...]).astype(BF16)
        rf = inverse_rms(value)
        d_normed = acc_back[...]
        scaled = d_normed * gain
        d_mixed = (
            ct.astype(F32)
            + rf * scaled
            - value * (rf * rf * rf) * jnp.mean(scaled * value, axis=-1, keepdims=True)
        )
        dgain_ref[...] = jnp.sum(d_normed * value * rf, axis=0, keepdims=True)
        dmix_ref[...] = d_mixed
        branch = d_mixed.astype(BF16)
        datt_ref[...] = dot_nt(branch, wo[...]).astype(BF16)
        for c in range(width // COLS):
            go_ref[c] = dot_tn(att_ref[...], branch[:, c * COLS : (c + 1) * COLS]).astype(BF16)


def feed(plan, x, attended, ct, gains, gate_up, pieces):
    tokens, width = x.shape
    ff = gate_up.shape[1] // 2
    steps = ff // COLS
    const = lambda *block: pl.BlockSpec(block, lambda j: (0,) * len(block))
    if plan.fast:
        lead = (plan.n_dp, plan.n_key // 2)
        rows = width // (plan.n_dp * plan.n_key)
    else:
        lead, rows = (1, 1), width
    grads = jax.ShapeDtypeStruct(lead + (2, rows, ff), BF16)
    return pl.pallas_call(
        functools.partial(feed_kernel, plan, len(pieces)),
        grid=(steps,),
        in_specs=[const(tokens, width)] * 3
        + [
            const(2, width),
            pl.BlockSpec((width, COLS), lambda j: (0, j)),
            pl.BlockSpec((width, COLS), lambda j: (0, j + steps)),
        ]
        + [pl.BlockSpec(memory_space=pl.ANY)] * len(pieces),
        out_specs=[pl.BlockSpec(lead + (2, rows, COLS), lambda j: (0, 0, 0, 0, j))] * plan.halves
        + [
            pl.BlockSpec((width // COLS, COLS, COLS), lambda j: (0, j, 0)),
            const(width // COLS, width, COLS),
            const(tokens, width),
            const(tokens, width),
            const(tokens, width),
            const(1, width),
        ],
        out_shape=[grads] * plan.halves
        + [
            jax.ShapeDtypeStruct((width // COLS, ff, COLS), BF16),
            jax.ShapeDtypeStruct((width // COLS, width, COLS), BF16),
            jax.ShapeDtypeStruct((tokens, width), BF16),
            jax.ShapeDtypeStruct((tokens, width), F32),
            jax.ShapeDtypeStruct((tokens, width), BF16),
            jax.ShapeDtypeStruct((1, width), F32),
        ],
        scratch_shapes=[
            pltpu.VMEM((width, width), BF16),
            pltpu.VMEM((ff, width), BF16),
            pltpu.VMEM((tokens, width), F32),
            pltpu.VMEM((tokens, width), BF16),
            pltpu.VMEM((plan.halves, width // plan.halves, tokens), BF16),
            pltpu.VMEM((tokens, width), F32),
            pltpu.VMEM((tokens, width), F32),
            pltpu.SemaphoreType.DMA((2,)),
        ],
        compiler_params=pltpu.CompilerParams(vmem_limit_bytes=VMEM_LIMIT),
        cost_estimate=pl.CostEstimate(
            flops=18 * tokens * width * ff, bytes_accessed=48 * 2**20, transcendentals=tokens * ff
        ),
        name="feed",
    )(x, attended, ct, gains, gate_up, gate_up, *pieces)


def attend_back_kernel(
    p_loc, p_mem, datt, att, qloc, kloc, v, memory, cos_ref, sin_ref, dq_ref, dk_ref, dv_ref
):
    mem_k, mem_v = memory_of(memory)
    grad = datt[...]
    delta = jnp.sum(grad.astype(F32) * att[...].astype(F32), axis=-1, keepdims=True)
    low_loc = p_loc[0]
    ds_loc = (low_loc.astype(F32) * (dot_nt(grad, v[...]) - delta)).astype(BF16)
    ds_mem = (p_mem[0].astype(F32) * (dot_nt(grad, mem_v) - delta)).astype(BF16)
    cosine, sine = cos_ref[...], sin_ref[...]
    dq_loc = dot(ds_loc, kloc[...]) * SCALE
    dq_mem = dot(ds_mem, mem_k) * SCALE
    dk = dot_tn(ds_loc, qloc[...]) * SCALE
    dq_ref[...] = (dq_mem + turn(dq_loc, cosine, -sine)).astype(BF16)
    dk_ref[...] = turn(dk, cosine, -sine).astype(BF16)
    dv_ref[...] = dot_tn(low_loc, grad).astype(BF16)


def attend_back(p_loc, p_mem, datt, att, qloc, kloc, v, memory, cosine, sine):
    tokens, width = datt.shape
    keys = p_mem.shape[2]
    head = pl.BlockSpec((tokens, HD), lambda h: (0, h))
    table = pl.BlockSpec((tokens, HD), lambda h: (0, 0))
    return pl.pallas_call(
        attend_back_kernel,
        grid=(width // HD,),
        in_specs=[
            pl.BlockSpec((1, tokens, tokens), lambda h: (h, 0, 0)),
            pl.BlockSpec((1, tokens, keys), lambda h: (h, 0, 0)),
        ]
        + [head] * 5
        + [pl.BlockSpec(memory.shape[:2] + (HD,), lambda h: (0, 0, h)), table, table],
        out_specs=[head] * 3,
        out_shape=[jax.ShapeDtypeStruct((tokens, width), BF16)] * 3,
        compiler_params=pltpu.CompilerParams(vmem_limit_bytes=VMEM_LIMIT),
        cost_estimate=pl.CostEstimate(
            flops=4 * tokens * (2 * tokens + keys) * width,
            bytes_accessed=24 * 2**20,
            transcendentals=0,
        ),
        name="attend_back",
    )(p_loc, p_mem, datt, att, qloc, kloc, v, memory, cosine, sine)


def project_back_kernel(plan, n_pieces, x_ref, normed_ref, dmix_ref, gains_ref, dgain_ref, dq, dk, dv, *refs):
    pieces, refs = refs[:n_pieces], refs[n_pieces:]
    n_half = plan.halves
    g_refs, refs = refs[:n_half], refs[n_half:]
    xgrad_ref, again_ref, w_ref, turned, sems = refs
    width = x_ref.shape[1]
    if plan.fast:
        rows = width // plan.n_key
        for m in range(3):
            for copy in place(plan, pieces, GAIN_ROWS + m * rows, rows, w_ref.at[m], sems.at[0]):
                copy.start()
    else:
        pltpu.make_async_copy(pieces[0], w_ref, sems.at[0]).start()
    store_turned(plan, normed_ref[...], turned, True)
    low = (dq, dk, dv)
    for half in range(n_half):
        rows = g_refs[half].shape[2] - GAIN_ROWS
        each = rows // 3
        lead = g_refs[half].shape[:2]
        for m in range(3):
            for c in range(width // COLS):
                cols = slice(c * COLS, (c + 1) * COLS)
                value = dot(turned[half], low[m][:, cols]).astype(BF16)
                g_refs[half][:, :, m * each : (m + 1) * each, cols] = value.reshape(
                    lead + (each, COLS)
                )
    pltpu.make_async_copy(w_ref, w_ref, sems.at[0]).wait()
    d_normed = dot_nt(dq[...], w_ref[0]) + dot_nt(dk[...], w_ref[1]) + dot_nt(dv[...], w_ref[2])
    x = x_ref[...].astype(F32)
    ra = inverse_rms(x)
    scaled = d_normed * gains_ref[0:1, :]
    xgrad_ref[...] = (
        dmix_ref[...]
        + ra * scaled
        - x * (ra * ra * ra) * jnp.mean(scaled * x, axis=-1, keepdims=True)
    )
    attn = jnp.sum(d_normed * x * ra, axis=0, keepdims=True)
    ffn = dgain_ref[...]
    again_ref[0:1, :] = attn
    again_ref[1:2, :] = ffn
    if plan.fast:
        key = lax.axis_index("key")
        core, z = lax.rem(key, 2), key // 2
        span = width // plan.n_key
        fill = jnp.zeros((1, width - 2 * span), F32)
        for zz in range(4):
            both = [
                jnp.concatenate(
                    [
                        attn[:, (zz * 2 + c) * span : (zz * 2 + c + 1) * span],
                        ffn[:, (zz * 2 + c) * span : (zz * 2 + c + 1) * span],
                        fill,
                    ],
                    axis=1,
                )
                for c in range(2)
            ]
            for half in range(2):
                row = jnp.where(core == half, both[0], both[1])
                tile = jnp.broadcast_to(row, (GAIN_ROWS, width)).astype(BF16)
                top = g_refs[half].shape[2] - GAIN_ROWS
                for far in range(4):
                    g_refs[half][far, z ^ zz, top:, :] = tile


def project_back(plan, x, normed, dmix, gains, dgain, dq, dk, dv, pieces):
    tokens, width = x.shape
    whole = pl.BlockSpec(memory_space=pltpu.VMEM)
    if plan.fast:
        lead = (plan.n_dp, plan.n_key // 2)
        rows = width // (plan.n_dp * plan.n_key)
    else:
        lead, rows = (1, 1), width
    grads = jax.ShapeDtypeStruct(lead + (3 * rows + GAIN_ROWS, width), BF16)
    return pl.pallas_call(
        functools.partial(project_back_kernel, plan, len(pieces)),
        in_specs=[whole] * 8 + [pl.BlockSpec(memory_space=pl.ANY)] * len(pieces),
        out_specs=[whole] * (plan.halves + 2),
        out_shape=[grads] * plan.halves
        + [
            jax.ShapeDtypeStruct((tokens, width), F32),
            jax.ShapeDtypeStruct((2, width), F32),
        ],
        scratch_shapes=[
            pltpu.VMEM((3, width, width), BF16),
            pltpu.VMEM((plan.halves, width // plan.halves, tokens), BF16),
            pltpu.SemaphoreType.DMA((1,)),
        ],
        compiler_params=pltpu.CompilerParams(vmem_limit_bytes=VMEM_LIMIT),
        cost_estimate=pl.CostEstimate(
            flops=12 * tokens * width * width, bytes_accessed=24 * 2**20, transcendentals=0
        ),
        name="project_back",
    )(x, normed, dmix, gains, dgain, dq, dk, dv, *pieces)


def add(*parts):
    total = parts[0].astype(F32)
    for part in parts[1:]:
        total = total + part.astype(F32)
    return total.astype(BF16)


def own_rows(natural, blocks, core):
    split = natural.reshape(natural.shape[0], blocks // 2, 2, -1, natural.shape[2])
    return lax.dynamic_index_in_dim(split, core, 2, keepdims=False)


def offloaded_sum(share):
    groups = [[0, 2, 4, 6], [1, 3, 5, 7]]
    share = lax.psum_scatter(share, "dp", scatter_dimension=0, tiled=False)
    share = lax.psum_scatter(
        share, "key", scatter_dimension=0, tiled=False, axis_index_groups=groups
    )
    return lax.all_gather(share, "dp", axis=0)


def swapped_sum(share):
    share = add(share[0], *[swap(share[r], "dp", 4, r) for r in (1, 2, 3)])
    share = add(share[0], *[swap(share[r], "key", 8, 2 * r) for r in (1, 2, 3)])
    held = jnp.stack([share] + [swap(share, "dp", 4, r) for r in (1, 2, 3)])
    return jnp.take(held, jnp.arange(4) ^ lax.axis_index("dp"), axis=0)


def per_device(
    plan,
    inputs,
    positions,
    memory_flag,
    partner,
    cache_keys,
    cache_values,
    query_proj,
    key_proj,
    value_proj,
    out_proj,
    gate_proj,
    up_proj,
    down_proj,
    attn_gain,
    ffn_gain,
    cotangent,
):
    x, ct, token_pos = inputs[0], cotangent[0], positions[0]
    tokens, width = x.shape
    group, slots = cache_keys.shape[0], cache_keys.shape[1]
    key = lax.axis_index("key")
    n_dp = plan.n_dp

    half = HD // 2
    frequency = ROPE_BASE ** (-2.0 * jnp.arange(half, dtype=F32) / HD)
    angles = token_pos.astype(F32)[:, None] * frequency[None, :]
    cosine, sine = jnp.cos(angles), jnp.sin(angles)
    cosine = jnp.concatenate([cosine, cosine], axis=1)
    sine = jnp.concatenate([-sine, sine], axis=1)
    order = jnp.arange(tokens, dtype=jnp.int32)
    valid = (order[None, :] <= order[:, None]) & (
        token_pos[:, None] - token_pos[None, :] == order[:, None] - order[None, :]
    )
    local_bias = jnp.where(valid, 0.0, NEG_FILL).astype(F32)
    self_flag = jnp.take(memory_flag, key)
    place_in_slot = jnp.arange(group * 2 * slots, dtype=jnp.int32) % (2 * slots)
    memory_bias = jnp.where((place_in_slot >= slots) | (self_flag == 1), 0.0, NEG_FILL)
    memory_bias = memory_bias.astype(F32)[None, :]

    outgoing = jnp.concatenate(
        [
            cache_keys,
            jnp.take(cache_keys, partner, axis=0),
            cache_values,
            jnp.take(cache_values, partner, axis=0),
        ],
        axis=1,
    )
    gate_up = jnp.concatenate([gate_proj, up_proj], axis=1)
    if plan.fast:
        share = gate_up.shape[0] // n_dp
        gate_up = lax.dynamic_slice_in_dim(gate_up, lax.axis_index("dp") * share, share, 0)
        gate_up = lax.all_gather(gate_up, ("key", "dp"), axis=0, tiled=True)
        gains = jnp.concatenate([attn_gain, ffn_gain])[None, :]
        first = along_z(
            jnp.concatenate(
                [jnp.broadcast_to(gains, (GAIN_ROWS, COLS))]
                + [own_quarter(w, n_dp) for w in (query_proj, key_proj, value_proj)],
                axis=0,
            )
        )
        second = jnp.concatenate([own_quarter(w, n_dp) for w in (out_proj, down_proj)], axis=0)
        outgoing, second = after((outgoing, second), first)
        first = across(first)
        first = first + other_core(first)
        second = across(along_z(second))
        second = second + other_core(second)
    else:
        whole = lambda w: lax.all_gather(w, "key", axis=0, tiled=True)
        gate_up = whole(gate_up)
        first = [
            jnp.stack([whole(query_proj), whole(key_proj), whole(value_proj)]),
            jnp.stack([whole(attn_gain), whole(ffn_gain)]).astype(F32),
        ]
        second = [whole(out_proj), whole(down_proj)]
    memory = lax.all_to_all(outgoing, "key", split_axis=0, concat_axis=0, tiled=True)

    qmem, qloc, kloc, kraw, v, normed, gains = project(plan, x, cosine, sine, first)
    attended, p_loc, p_mem = attend(qmem, qloc, kloc, v, memory, local_bias, memory_bias)

    run = tokens // group
    fresh = jnp.stack([kraw.reshape(group, run, width), v.reshape(group, run, width)], axis=1)
    fresh = after(fresh, attended)
    arrived = lax.all_to_all(fresh, "key", split_axis=0, concat_axis=0, tiled=True)
    new_keys = jnp.concatenate([cache_keys[:, run:], arrived[:, 0]], axis=1)
    new_values = jnp.concatenate([cache_values[:, run:], arrived[:, 1]], axis=1)

    *g_gu, g_down, g_out, outputs, dmix, datt, dgain = feed(
        plan, x, attended, ct, gains, gate_up, second
    )
    dq, dk, dv = attend_back(p_loc, p_mem, datt, attended, qloc, kloc, v, memory, cosine, sine)
    *g_qkv, input_grad, gain_grads = project_back(
        plan, x, normed, dmix, gains, dgain, dq, dk, dv, first[:8] if plan.fast else first[:1]
    )

    rows = width // plan.n_key
    if plan.fast:
        core = lax.rem(key, 2)
        g_gu = offloaded_sum(add(g_gu[0], swap(g_gu[1], "key", 8, 1)))
        natural = (g_down, g_out)
        mine = jnp.concatenate([own_rows(g, 8, core) for g in natural], axis=2)
        other = jnp.concatenate([own_rows(g, 8, 1 - core) for g in natural], axis=2)
        g_do = offloaded_sum(add(mine, swap(other, "key", 8, 1)))
        g_do = g_do.transpose(1, 0, 2).reshape(-1, width).astype(F32)
        total_down, total_out = g_do[:-rows], g_do[-rows:]
        total_gate = g_gu[:, 0].reshape(rows, -1).astype(F32)
        total_up = g_gu[:, 1].reshape(rows, -1).astype(F32)
        g_qkv = swapped_sum(add(g_qkv[0], swap(g_qkv[1], "key", 8, 1))).astype(F32)
        each = rows // n_dp
        total_query, total_key, total_value = (
            g_qkv[:, m * each : (m + 1) * each].reshape(rows, width) for m in range(3)
        )
        total_attn, total_ffn = g_qkv[0, 3 * each, :rows], g_qkv[0, 3 * each, rows : 2 * rows]
    else:

        def total(g):
            g = lax.psum_scatter(g.astype(F32), "key", scatter_dimension=0, tiled=True)
            return lax.psum(g.astype(BF16), "dp").astype(F32)

        wide = lambda g: g.transpose(1, 0, 2).reshape(g.shape[1], width)
        total_query, total_key, total_value = (
            total(g_qkv[0][0, 0, m * width : (m + 1) * width]) for m in range(3)
        )
        total_gate, total_up = total(g_gu[0][0, 0, 0]), total(g_gu[0][0, 0, 1])
        total_down, total_out = total(wide(g_down)), total(wide(g_out))
        total_attn, total_ffn = total(gain_grads[0]), total(gain_grads[1])
    return (
        outputs[None],
        input_grad[None],
        total_query,
        total_key,
        total_value,
        total_out,
        total_gate,
        total_up,
        total_down,
        total_attn,
        total_ffn,
        new_keys,
        new_values,
    )


def solution(mesh):
    plan = Plan(mesh.shape["dp"], mesh.shape["key"])
    rows, cache = P(("dp", "key"), None, None), P("dp", "key", None)
    weight, gain = P("key", None), P("key")
    return jax.shard_map(
        functools.partial(per_device, plan),
        mesh=mesh,
        in_specs=(rows, P(("dp", "key"), None), P("dp"), P("dp"), cache, cache)
        + (weight,) * 7
        + (gain, gain, rows),
        out_specs=(rows, rows) + (weight,) * 7 + (gain, gain, cache, cache),
        check_vma=False,
    )
```

```python
import functools
import math

import jax
import jax.numpy as jnp
from jax import lax
from jax.experimental import pallas as pl
from jax.experimental.pallas import tpu as pltpu
from jax.sharding import PartitionSpec as P

H = 8
HD = 128
EPSILON = 1e-05
ROPE_BASE = 10000.0
NEG_FILL = -1e30
SCALE = 1.0 / math.sqrt(HD)
BF16 = jnp.bfloat16
F32 = jnp.float32
COLS = 256
GAIN_ROWS = 16
KEY = ("z", "core")
VMEM_LIMIT = 58 * 1024 * 1024


def dot(left, right):
    return jnp.dot(left, right, preferred_element_type=F32)


def dot_nt(left, right):
    return lax.dot_general(left, right, (((1,), (1,)), ((), ())), preferred_element_type=F32)


def dot_tn(left, right):
    return lax.dot_general(left, right, (((0,), (0,)), ((), ())), preferred_element_type=F32)


def inverse_rms(values):
    return lax.rsqrt(jnp.mean(values * values, axis=-1, keepdims=True) + EPSILON)


def turn(values, cosine, sine):
    return values * cosine + pltpu.roll(values, HD // 2, 1) * sine


def cost(flops):
    return pl.CostEstimate(flops=flops, bytes_accessed=24 * 2**20, transcendentals=0)


class Plan:
    def __init__(self, n_dp, n_key):
        self.n_dp, self.n_key = n_dp, n_key
        self.fast = n_dp == 4 and n_key == 8
        self.halves = 2 if self.fast else 1


def swap(values, axis, size, distance):
    return lax.ppermute(values, axis, [(i, i ^ distance) for i in range(size)])


def own_quarter(weight, n_dp):
    width = weight.shape[1] // n_dp
    return lax.dynamic_slice_in_dim(weight, lax.axis_index("dp") * width, width, 1)


def along_z(quarter):
    return [quarter] + [swap(quarter, KEY, 8, 2 * r) for r in (1, 2, 3)]


def across(held):
    x, y = swap(held, "dp", 4, 1), swap(held, "dp", 4, 2)
    return [held, x, y, swap(x[:2], "dp", 4, 2), swap(y[2:], "dp", 4, 1)]


def other_core(pieces):
    return [swap(piece, KEY, 8, 1) for piece in pieces]


def after(values, token):
    return lax.optimization_barrier((values, token))[0]


def place(plan, pieces, first_row, rows, target, sem):
    copies = []
    q, key = lax.axis_index("dp"), lax.axis_index(KEY)
    for core in range(2):
        own, x, y, far_low, far_high = pieces[core * 5 : core * 5 + 5]
        for far in range(4):
            for zr in range(4):
                if far < 3:
                    source = (own, x, y)[far].at[zr]
                else:
                    source = far_low.at[zr] if zr < 2 else far_high.at[zr - 2]
                row = pl.multiple_of((key ^ (2 * zr + core)) * rows, 16)
                column = pl.multiple_of((q ^ far) * COLS, COLS)
                copies.append(
                    pltpu.make_async_copy(
                        source.at[pl.ds(first_row, rows)],
                        target.at[pl.ds(row, rows), pl.ds(column, COLS)],
                        sem,
                    )
                )
    return copies


def place_rows(plan, held, target, sem):
    z = lax.axis_index("z")
    rows = held.shape[3]
    return [
        pltpu.make_async_copy(
            held.at[far, core, zr],
            target.at[
                pl.ds(pl.multiple_of((((z ^ zr) * 2 + core) * 4 + far) * rows, 16), rows)
            ],
            sem,
        )
        for core in range(2)
        for far in range(4)
        for zr in range(4)
    ]


def slot(far, zr):
    half = zr // 2
    return half, ((0, 1, 2, 3), (0, 2, 1, 3))[half][far], zr % 2


def store_turned(plan, values, flat, target, relative):
    if not plan.fast:
        target[...] = values.T.reshape(target.shape)
        return
    flat[...] = values.T
    q, key = lax.axis_index("dp"), lax.axis_index(KEY)
    z = lax.axis_index("z")
    rows = flat.shape[0] // 32
    for core in range(2):
        for far in range(4):
            for zr in range(4):
                if relative:
                    block = (key ^ (2 * zr + core)) * 4 + (q ^ far)
                    half, pos, low = slot(far, zr)
                    row = ((half * 4 + pos) * 2 + low) * rows
                    place_at = (core, slice(row, row + rows))
                else:
                    block = ((z ^ zr) * 2 + core) * 4 + far
                    row = ((far * 2 + core) * 4 + zr) * rows
                    place_at = slice(row, row + rows)
                target[place_at] = flat[pl.ds(pl.multiple_of(block * rows, rows), rows), :]


def project_kernel(plan, n_pieces, x_ref, cos_ref, sin_ref, *refs):
    pieces, refs = refs[:n_pieces], refs[n_pieces:]
    qmem_ref, qloc_ref, kloc_ref, kraw_ref, v_ref, normed_ref, gains_ref, w_ref, g_ref, sems = refs
    width = x_ref.shape[1]
    if plan.fast:
        rows = width // plan.n_key
        copies = []
        for m in range(3):
            copies += place(plan, pieces, GAIN_ROWS + m * rows, rows, w_ref.at[m], sems.at[0])
        key = lax.axis_index(KEY)
        for core in range(2):
            for zr in range(4):
                copies.append(
                    pltpu.make_async_copy(
                        pieces[core * 5].at[zr, pl.ds(0, GAIN_ROWS)],
                        g_ref.at[key ^ (2 * zr + core)],
                        sems.at[1],
                    )
                )
        for copy in copies:
            copy.start()
        pltpu.make_async_copy(g_ref, g_ref, sems.at[1]).wait()
        lead = [g_ref[k][0:1, :].astype(F32) for k in range(plan.n_key)]
        attn_gain = jnp.concatenate([row[:, :rows] for row in lead], axis=1)
        ffn_gain = jnp.concatenate([row[:, rows:] for row in lead], axis=1)
    else:
        copy = pltpu.make_async_copy(pieces[0], w_ref, sems.at[0])
        copy.start()
        attn_gain = pieces[1][0:1, :]
        ffn_gain = pieces[1][1:2, :]
    gains_ref[0:1, :] = attn_gain
    gains_ref[1:2, :] = ffn_gain
    x = x_ref[...].astype(F32)
    normed = (x * inverse_rms(x) * attn_gain).astype(BF16)
    normed_ref[...] = normed
    pltpu.make_async_copy(w_ref, w_ref, sems.at[0]).wait()
    cosine, sine = cos_ref[...], sin_ref[...]
    for m in range(3):
        for c in range(width // COLS):
            cols = slice(c * COLS, (c + 1) * COLS)
            raw = dot(normed, w_ref[m, :, cols])
            low = raw.astype(BF16)
            if m == 2:
                v_ref[:, cols] = low
                continue
            (qmem_ref if m == 0 else kraw_ref)[:, cols] = low
            out = qloc_ref if m == 0 else kloc_ref
            for h in range(COLS // HD):
                part = raw[:, h * HD : (h + 1) * HD]
                start = c * COLS + h * HD
                out[:, start : start + HD] = turn(part, cosine, sine).astype(BF16)


def project(plan, x, cosine, sine, pieces):
    tokens, width = x.shape
    whole = pl.BlockSpec(memory_space=pltpu.VMEM)
    anywhere = pl.BlockSpec(memory_space=pl.ANY)
    row = jax.ShapeDtypeStruct((tokens, width), BF16)
    return pl.pallas_call(
        functools.partial(project_kernel, plan, len(pieces)),
        out_shape=[row] * 6 + [jax.ShapeDtypeStruct((2, width), F32)],
        in_specs=[whole] * 3 + ([anywhere] * len(pieces) if plan.fast else [anywhere, whole]),
        out_specs=[whole] * 7,
        scratch_shapes=[
            pltpu.VMEM((3, width, width), BF16),
            pltpu.VMEM((plan.n_key, GAIN_ROWS, COLS), BF16),
            pltpu.SemaphoreType.DMA((2,)),
        ],
        compiler_params=pltpu.CompilerParams(vmem_limit_bytes=VMEM_LIMIT),
        cost_estimate=cost(6 * tokens * width * width),
        name="project",
    )(x, cosine, sine, *pieces)


def flat_rows(ref):
    block = ref[...]
    return block.reshape(block.shape[0] * block.shape[1], block.shape[2])


def weigh_kernel(qmem, qloc, kloc, mem_k, local_bias, memory_bias, p_loc, p_mem):
    s_loc = dot_nt(qloc[...], kloc[...]) * SCALE + local_bias[...]
    s_mem = dot_nt(qmem[...], flat_rows(mem_k)) * SCALE + memory_bias[...]
    largest = jnp.maximum(
        jnp.max(s_loc, axis=-1, keepdims=True), jnp.max(s_mem, axis=-1, keepdims=True)
    )
    e_loc = jnp.exp(s_loc - largest)
    e_mem = jnp.exp(s_mem - largest)
    total = jnp.sum(e_loc, axis=-1, keepdims=True) + jnp.sum(e_mem, axis=-1, keepdims=True)
    inverse = 1.0 / total
    p_loc[0] = (e_loc * inverse).astype(BF16)
    p_mem[0] = (e_mem * inverse).astype(BF16)


def head_spec(tokens):
    return pl.BlockSpec((tokens, HD), lambda h: (0, h))


def memory_spec(memory):
    return pl.BlockSpec(memory.shape[:2] + (HD,), lambda h: (0, 0, h))


def prob_specs(tokens, keys):
    return [
        pl.BlockSpec((1, tokens, tokens), lambda h: (h, 0, 0)),
        pl.BlockSpec((1, tokens, keys), lambda h: (h, 0, 0)),
    ]


def weigh(qmem, qloc, kloc, mem_k, local_bias, memory_bias):
    tokens, width = qmem.shape
    keys = memory_bias.shape[1]
    return pl.pallas_call(
        weigh_kernel,
        grid=(width // HD,),
        in_specs=[head_spec(tokens)] * 3
        + [
            memory_spec(mem_k),
            pl.BlockSpec((tokens, tokens), lambda h: (0, 0)),
            pl.BlockSpec((1, keys), lambda h: (0, 0)),
        ],
        out_specs=prob_specs(tokens, keys),
        out_shape=[
            jax.ShapeDtypeStruct((width // HD, tokens, tokens), BF16),
            jax.ShapeDtypeStruct((width // HD, tokens, keys), BF16),
        ],
        compiler_params=pltpu.CompilerParams(vmem_limit_bytes=VMEM_LIMIT),
        cost_estimate=cost(4 * tokens * (tokens + keys) * width),
        name="weigh",
    )(qmem, qloc, kloc, mem_k, local_bias, memory_bias)


def attend_kernel(p_loc, p_mem, v, mem_v, out):
    out[...] = (dot(p_loc[0], v[...]) + dot(p_mem[0], flat_rows(mem_v))).astype(BF16)


def attend(p_loc, p_mem, v, mem_v):
    tokens, width = v.shape
    keys = p_mem.shape[2]
    return pl.pallas_call(
        attend_kernel,
        grid=(width // HD,),
        in_specs=prob_specs(tokens, keys) + [head_spec(tokens), memory_spec(mem_v)],
        out_specs=head_spec(tokens),
        out_shape=jax.ShapeDtypeStruct((tokens, width), BF16),
        compiler_params=pltpu.CompilerParams(vmem_limit_bytes=VMEM_LIMIT),
        cost_estimate=cost(2 * tokens * (tokens + keys) * width),
        name="attend",
    )(p_loc, p_mem, v, mem_v)


def feed_kernel(plan, n_pieces, x_ref, att_ref, ct_ref, gains_ref, *refs):
    pieces, refs = refs[:n_pieces], refs[n_pieces:]
    n_half = plan.halves
    gu_ref, do_refs, refs = refs[0], refs[1 : 1 + n_half], refs[1 + n_half :]
    out_ref, dmix_ref, datt_ref = refs[:3]
    wo, wd, wgu, mixed, normed, flat, turned, acc_out, acc_back, g_down, g_out, sems = refs[3:]
    step = pl.program_id(0)
    tokens, width = x_ref.shape
    ff = wd.shape[0]
    gain = gains_ref[1:2, :]

    @pl.when(step == 0)
    def _():
        if plan.fast:
            rows = width // plan.n_key
            copies = place(plan, pieces, 0, rows, wo, sems.at[0])
            copies += place_rows(plan, pieces[-1], wgu, sems.at[1])
            copies += place(plan, pieces, rows, ff // plan.n_key, wd, sems.at[2])
        else:
            copies = [
                pltpu.make_async_copy(piece, held, sems.at[i])
                for i, (piece, held) in enumerate(zip(pieces, (wo, wgu, wd)))
            ]
        for copy in copies:
            copy.start()
        pltpu.make_async_copy(wo, wo, sems.at[0]).wait()
        mixed[...] = x_ref[...].astype(F32) + dot(att_ref[...], wo[...])
        value = mixed[...]
        low = (value * inverse_rms(value) * gain).astype(BF16)
        normed[...] = low
        store_turned(plan, low, flat, turned, False)
        acc_out[...] = jnp.zeros_like(acc_out)
        acc_back[...] = jnp.zeros_like(acc_back)
        pltpu.make_async_copy(wgu, wgu, sems.at[1]).wait()
        pltpu.make_async_copy(wd, wd, sems.at[2]).wait()

    ct = ct_ref[...]
    first = pl.multiple_of(step * COLS, COLS)
    down = wd[pl.ds(first, COLS), :]
    w_gate = wgu[:, pl.ds(first, COLS)]
    w_up = wgu[:, pl.ds(first + ff, COLS)]
    gate = dot(normed[...], w_gate)
    up = dot(normed[...], w_up)
    back = dot_nt(ct, down)
    sigma = 1.0 / (1.0 + jnp.exp(-gate))
    swish = gate * sigma
    hidden = (swish * up).astype(BF16)
    d_gate = (back * up * (sigma * (1.0 + gate * (1.0 - sigma)))).astype(BF16)
    d_up = (back * swish).astype(BF16)
    acc_out[...] += dot(hidden, down)
    acc_back[...] += dot_nt(d_gate, w_gate) + dot_nt(d_up, w_up)
    grad_down = dot_tn(hidden, ct).astype(BF16)
    for c in range(width // COLS):
        g_down[c, pl.ds(first, COLS), :] = grad_down[:, c * COLS : (c + 1) * COLS]
    lead = gu_ref.shape[:3]
    for i, grad in enumerate((d_gate, d_up)):
        value = dot(turned[...], grad).astype(BF16)
        gu_ref[:, :, :, i] = value.reshape(lead + (-1, COLS))

    @pl.when(step == pl.num_programs(0) - 1)
    def _():
        copies = []

        def send(source, offset):
            if not plan.fast:
                n = source.shape[1]
                for c in range(width // COLS):
                    copies.append(
                        pltpu.make_async_copy(
                            source.at[c], do_refs[0].at[c, pl.ds(offset, n)], sems.at[0]
                        )
                    )
            else:
                q, key = lax.axis_index("dp"), lax.axis_index(KEY)
                n = source.shape[1] // plan.n_key
                for core in range(2):
                    for far in range(4):
                        for zr in range(4):
                            row = pl.multiple_of((key ^ (2 * zr + core)) * n, 16)
                            copies.append(
                                pltpu.make_async_copy(
                                    source.at[q ^ far, pl.ds(row, n)],
                                    do_refs[core].at[slot(far, zr)].at[pl.ds(offset, n)],
                                    sems.at[0],
                                )
                            )

        send(g_down, 0)
        for copy in copies:
            copy.start()
        value = mixed[...]
        out_ref[...] = (value + acc_out[...]).astype(BF16)
        rf = inverse_rms(value)
        d_normed = acc_back[...]
        scaled = d_normed * gain
        d_mixed = (
            ct.astype(F32)
            + rf * scaled
            - value * (rf * rf * rf) * jnp.mean(scaled * value, axis=-1, keepdims=True)
        )
        dmix_ref[...] = d_mixed
        branch = d_mixed.astype(BF16)
        for c in range(width // COLS):
            g_out[c] = dot_tn(att_ref[...], branch[:, c * COLS : (c + 1) * COLS]).astype(BF16)
        started = len(copies)
        send(g_out, (ff if not plan.fast else ff // plan.n_key))
        for copy in copies[started:]:
            copy.start()
        datt_ref[...] = dot_nt(branch, wo[...]).astype(BF16)
        for copy in copies:
            copy.wait()


def feed(plan, x, attended, ct, gains, pieces, ff):
    tokens, width = x.shape
    steps = ff // COLS
    const = lambda *block: pl.BlockSpec(block, lambda j: (0,) * len(block))
    anywhere = pl.BlockSpec(memory_space=pl.ANY)
    if plan.fast:
        lead = (plan.n_dp, 2, plan.n_key // 2)
        rows = width // (plan.n_dp * plan.n_key)
        do_shape = (2, 4, 2, (ff + width) // plan.n_key, COLS)
    else:
        lead, rows = (1, 1, 1), width
        do_shape = (width // COLS, ff + width, COLS)
    return pl.pallas_call(
        functools.partial(feed_kernel, plan, len(pieces)),
        grid=(steps,),
        in_specs=[const(tokens, width)] * 3 + [const(2, width)] + [anywhere] * len(pieces),
        out_specs=[pl.BlockSpec(lead + (2, rows, COLS), lambda j: (0, 0, 0, 0, 0, j))]
        + [anywhere] * plan.halves
        + [const(tokens, width)] * 3,
        out_shape=[jax.ShapeDtypeStruct(lead + (2, rows, ff), BF16)]
        + [jax.ShapeDtypeStruct(do_shape, BF16)] * plan.halves
        + [
            jax.ShapeDtypeStruct((tokens, width), BF16),
            jax.ShapeDtypeStruct((tokens, width), F32),
            jax.ShapeDtypeStruct((tokens, width), BF16),
        ],
        scratch_shapes=[
            pltpu.VMEM((width, width), BF16),
            pltpu.VMEM((ff, width), BF16),
            pltpu.VMEM((width, 2 * ff), BF16),
            pltpu.VMEM((tokens, width), F32),
            pltpu.VMEM((tokens, width), BF16),
            pltpu.VMEM((width, tokens), BF16),
            pltpu.VMEM((width, tokens), BF16),
            pltpu.VMEM((tokens, width), F32),
            pltpu.VMEM((tokens, width), F32),
            pltpu.VMEM((width // COLS, ff, COLS), BF16),
            pltpu.VMEM((width // COLS, width, COLS), BF16),
            pltpu.SemaphoreType.DMA((3,)),
        ],
        compiler_params=pltpu.CompilerParams(vmem_limit_bytes=VMEM_LIMIT),
        cost_estimate=cost(18 * tokens * width * ff),
        name="feed",
    )(x, attended, ct, gains, *pieces)


def attend_back_kernel(
    p_loc, p_mem, datt, att, qloc, kloc, v, mem_k, mem_v, cos_ref, sin_ref, dq_ref, dk_ref, dv_ref
):
    grad = datt[...]
    delta = jnp.sum(grad.astype(F32) * att[...].astype(F32), axis=-1, keepdims=True)
    low_loc = p_loc[0]
    ds_loc = (low_loc.astype(F32) * (dot_nt(grad, v[...]) - delta)).astype(BF16)
    ds_mem = (p_mem[0].astype(F32) * (dot_nt(grad, flat_rows(mem_v)) - delta)).astype(BF16)
    cosine, sine = cos_ref[...], sin_ref[...]
    dq_loc = dot(ds_loc, kloc[...]) * SCALE
    dq_mem = dot(ds_mem, flat_rows(mem_k)) * SCALE
    dk = dot_tn(ds_loc, qloc[...]) * SCALE
    dq_ref[...] = (dq_mem + turn(dq_loc, cosine, -sine)).astype(BF16)
    dk_ref[...] = turn(dk, cosine, -sine).astype(BF16)
    dv_ref[...] = dot_tn(low_loc, grad).astype(BF16)


def attend_back(p_loc, p_mem, datt, att, qloc, kloc, v, mem_k, mem_v, cosine, sine):
    tokens, width = datt.shape
    keys = p_mem.shape[2]
    table = pl.BlockSpec((tokens, HD), lambda h: (0, 0))
    return pl.pallas_call(
        attend_back_kernel,
        grid=(width // HD,),
        in_specs=prob_specs(tokens, keys)
        + [head_spec(tokens)] * 5
        + [memory_spec(mem_k), memory_spec(mem_v), table, table],
        out_specs=[head_spec(tokens)] * 3,
        out_shape=[jax.ShapeDtypeStruct((tokens, width), BF16)] * 3,
        compiler_params=pltpu.CompilerParams(vmem_limit_bytes=VMEM_LIMIT),
        cost_estimate=cost(4 * tokens * (2 * tokens + keys) * width),
        name="attend_back",
    )(p_loc, p_mem, datt, att, qloc, kloc, v, mem_k, mem_v, cosine, sine)


def project_grads_kernel(plan, normed_ref, dq, dk, dv, *refs):
    n_half = plan.halves
    g_refs, (flat, turned) = refs[:n_half], refs[n_half:]
    width = normed_ref.shape[1]
    store_turned(plan, normed_ref[...], flat, turned, True)
    low = (dq, dk, dv)
    for half in range(n_half):
        each = g_refs[half].shape[-2] // 3
        lead = g_refs[half].shape[:-2]
        for m in range(3):
            for c in range(width // COLS):
                cols = slice(c * COLS, (c + 1) * COLS)
                value = dot(turned[half], low[m][:, cols]).astype(BF16)
                g_refs[half][..., m * each : (m + 1) * each, cols] = value.reshape(
                    lead + (each, COLS)
                )


def project_grads(plan, normed, dq, dk, dv):
    tokens, width = normed.shape
    whole = pl.BlockSpec(memory_space=pltpu.VMEM)
    if plan.fast:
        lead, rows = (2, 4, 2), width // (plan.n_dp * plan.n_key)
    else:
        lead, rows = (1, 1), width
    return pl.pallas_call(
        functools.partial(project_grads_kernel, plan),
        in_specs=[whole] * 4,
        out_specs=[whole] * plan.halves,
        out_shape=[jax.ShapeDtypeStruct(lead + (3 * rows, width), BF16)] * plan.halves,
        scratch_shapes=[
            pltpu.VMEM((width, tokens), BF16),
            pltpu.VMEM((plan.halves, width // plan.halves, tokens), BF16),
        ],
        compiler_params=pltpu.CompilerParams(vmem_limit_bytes=VMEM_LIMIT),
        cost_estimate=cost(2**20),
        name="project_grads",
    )(normed, dq, dk, dv)


def project_back_kernel(plan, n_pieces, x_ref, dmix_ref, gains_ref, dq, dk, dv, *refs):
    pieces, refs = refs[:n_pieces], refs[n_pieces:]
    xgrad_ref, w_ref, sems = refs
    if plan.fast:
        rows = x_ref.shape[1] // plan.n_key
        for m in range(3):
            for copy in place(plan, pieces, GAIN_ROWS + m * rows, rows, w_ref.at[m], sems.at[0]):
                copy.start()
    else:
        pltpu.make_async_copy(pieces[0], w_ref, sems.at[0]).start()
    x = x_ref[...].astype(F32)
    ra = inverse_rms(x)
    pltpu.make_async_copy(w_ref, w_ref, sems.at[0]).wait()
    d_normed = dot_nt(dq[...], w_ref[0]) + dot_nt(dk[...], w_ref[1]) + dot_nt(dv[...], w_ref[2])
    scaled = d_normed * gains_ref[0:1, :]
    xgrad_ref[...] = (
        dmix_ref[...]
        + ra * scaled
        - x * (ra * ra * ra) * jnp.mean(scaled * x, axis=-1, keepdims=True)
    )


def project_back(plan, x, dmix, gains, dq, dk, dv, pieces):
    tokens, width = x.shape
    whole = pl.BlockSpec(memory_space=pltpu.VMEM)
    return pl.pallas_call(
        functools.partial(project_back_kernel, plan, len(pieces)),
        in_specs=[whole] * 6 + [pl.BlockSpec(memory_space=pl.ANY)] * len(pieces),
        out_specs=whole,
        out_shape=jax.ShapeDtypeStruct((tokens, width), F32),
        scratch_shapes=[pltpu.VMEM((3, width, width), BF16), pltpu.SemaphoreType.DMA((1,))],
        compiler_params=pltpu.CompilerParams(vmem_limit_bytes=VMEM_LIMIT),
        cost_estimate=cost(2**20),
        name="project_back",
    )(x, dmix, gains, dq, dk, dv, *pieces)


def add(*parts):
    total = parts[0].astype(F32)
    for part in parts[1:]:
        total = total + part.astype(F32)
    return total.astype(BF16)


def both_cores(own, other):
    return add(own, swap(other, KEY, 8, 1))


def over_dp_first(share, token=None):
    from_y = swap(share[0, 2:], "dp", 4, 2)
    from_x = swap(share[1, 2:], "dp", 4, 1)
    if token is not None:
        from_y, from_x = after((from_y, from_x), token)
    mine = share[0, 0], from_y[0], share[1, 0], from_x[0]
    return mine, (add(share[0, 1], from_y[1]), add(share[1, 1], from_x[1]))


def over_dp_second(mine, passed, token):
    low, high = swap(passed[0], "dp", 4, 1), swap(passed[1], "dp", 4, 2)
    low, high = after((low, high), token)
    low, high = add(*mine[:2], low), add(*mine[2:], high)
    return [low[0], low[1], high[0], high[1]]


def over_z(parts, token=None):
    come = [swap(parts[r], KEY, 8, 2 * r) for r in (1, 2, 3)]
    if token is not None:
        come = after(come, token)
    return add(parts[0], *come)


def from_dp(share):
    held = jnp.stack([share] + [swap(share, "dp", 4, r) for r in (1, 2, 3)])
    return jnp.take(held, jnp.arange(4) ^ lax.axis_index("dp"), axis=0)


def per_device(
    plan,
    inputs,
    positions,
    memory_flag,
    partner,
    cache_keys,
    cache_values,
    query_proj,
    key_proj,
    value_proj,
    out_proj,
    gate_proj,
    up_proj,
    down_proj,
    attn_gain,
    ffn_gain,
    cotangent,
):
    x, ct, token_pos = inputs[0], cotangent[0], positions[0]
    tokens, width = x.shape
    group, slots = cache_keys.shape[0], cache_keys.shape[1]
    key = lax.axis_index(KEY)
    n_dp = plan.n_dp

    half = HD // 2
    frequency = ROPE_BASE ** (-2.0 * jnp.arange(half, dtype=F32) / HD)
    angles = token_pos.astype(F32)[:, None] * frequency[None, :]
    cosine, sine = jnp.cos(angles), jnp.sin(angles)
    cosine = jnp.concatenate([cosine, cosine], axis=1)
    sine = jnp.concatenate([-sine, sine], axis=1)
    order = jnp.arange(tokens, dtype=jnp.int32)
    valid = (order[None, :] <= order[:, None]) & (
        token_pos[:, None] - token_pos[None, :] == order[:, None] - order[None, :]
    )
    local_bias = jnp.where(valid, 0.0, NEG_FILL).astype(F32)
    self_flag = jnp.take(memory_flag, key)
    place_in_slot = jnp.arange(group * 2 * slots, dtype=jnp.int32) % (2 * slots)
    memory_bias = jnp.where((place_in_slot >= slots) | (self_flag == 1), 0.0, NEG_FILL)
    memory_bias = memory_bias.astype(F32)[None, :]

    out_k, out_v = (
        jnp.concatenate([cache, jnp.take(cache, partner, axis=0)], axis=1)
        for cache in (cache_keys, cache_values)
    )
    rows = width // plan.n_key
    if plan.fast:
        gains = jnp.concatenate([attn_gain, ffn_gain])[None, :]
        project_in = jnp.concatenate(
            [jnp.broadcast_to(gains, (GAIN_ROWS, COLS))]
            + [own_quarter(w, n_dp) for w in (query_proj, key_proj, value_proj)],
            axis=0,
        )
        project_out = jnp.concatenate([own_quarter(w, n_dp) for w in (out_proj, down_proj)], axis=0)
        share = rows // n_dp
        gate_up = jnp.concatenate(
            [
                lax.dynamic_slice_in_dim(w, lax.axis_index("dp") * share, share, 0)
                for w in (gate_proj, up_proj)
            ],
            axis=1,
        )
        gate_up = along_z(gate_up)
        gate_up = after(gate_up, (project_in, project_out, out_k, out_v))
        project_in = along_z(after(project_in, gate_up))
        project_out = along_z(after(project_out, project_in))
        out_k = after(out_k, project_out)
        gate_up = lax.all_gather(jnp.stack(gate_up), ("dp", "core"), axis=0, tiled=False)
        gate_up = gate_up.reshape((n_dp, 2) + gate_up.shape[1:])
        project_in = across(jnp.stack(project_in))
        project_out = across(jnp.stack(after(project_out, project_in)))
        out_v = after(out_v, project_in)
        first = project_in + other_core(project_in)
        second = project_out + other_core(project_out) + [gate_up]
    else:
        whole = lambda w: lax.all_gather(w, KEY, axis=0, tiled=True)
        first = [
            jnp.stack([whole(query_proj), whole(key_proj), whole(value_proj)]),
            jnp.stack([whole(attn_gain), whole(ffn_gain)]).astype(F32),
        ]
        second = [
            whole(out_proj),
            whole(jnp.concatenate([gate_proj, up_proj], axis=1)),
            whole(down_proj),
        ]
    mem_k = lax.all_to_all(out_k, KEY, split_axis=0, concat_axis=0, tiled=True)
    out_v = after(out_v, mem_k)
    mem_v = lax.all_to_all(out_v, KEY, split_axis=0, concat_axis=0, tiled=True)

    qmem, qloc, kloc, kraw, v, normed, gains = project(plan, x, cosine, sine, first)
    p_loc, p_mem = weigh(qmem, qloc, kloc, mem_k, local_bias, memory_bias)
    attended = attend(p_loc, p_mem, v, mem_v)

    run = tokens // group
    fresh = jnp.stack([kraw.reshape(group, run, width), v.reshape(group, run, width)], axis=1)
    fresh = after(fresh, attended)
    arrived = lax.all_to_all(fresh, KEY, split_axis=0, concat_axis=0, tiled=True)
    new_keys = jnp.concatenate([cache_keys[:, run:], arrived[:, 0]], axis=1)
    new_values = jnp.concatenate([cache_values[:, run:], arrived[:, 1]], axis=1)

    n_half, ff = plan.halves, gate_proj.shape[1]
    results = feed(plan, x, attended, ct, gains, second, ff)
    g_gu, g_do, (outputs, dmix, datt) = (
        results[0],
        results[1 : 1 + n_half],
        results[1 + n_half :],
    )
    if plan.fast:
        g_gu = g_gu.reshape((8,) + g_gu.shape[2:])
        g_gu = lax.psum_scatter(g_gu, ("dp", "core"), scatter_dimension=0, tiled=True)
        g_gu = lax.optimization_barrier(g_gu)
    if plan.fast:
        g_do = both_cores(*g_do)
        datt = after(datt, g_do)
    dq, dk, dv = attend_back(
        p_loc, p_mem, datt, attended, qloc, kloc, v, mem_k, mem_v, cosine, sine
    )
    if plan.fast:
        do_mine, do_passed = over_dp_first(g_do, dq)
        dq = after(dq, do_passed)
    g_qkv = project_grads(plan, normed, dq, dk, dv)
    dq = after(dq, g_qkv)
    if plan.fast:
        do_blocks = over_dp_second(do_mine, do_passed, g_qkv)
        dq = after(dq, do_blocks)
    input_grad = project_back(
        plan, x, dmix, gains, dq, dk, dv, first if plan.fast else first[:1]
    )

    if plan.fast:
        own, swapped = g_qkv[0], swap(g_qkv[1], KEY, 8, 1)
        g_qkv = add(*after((own, swapped), (input_grad, arrived)))
        g_do = over_z(do_blocks, g_qkv)
        g_gu = after(g_gu, g_do)[0]
        mine, passed = over_dp_first(g_qkv, g_gu)
        g_gu = over_z(g_gu, passed)
        blocks = over_dp_second(mine, passed, g_gu)
        g_do = from_dp(g_do)
        g_qkv = over_z(blocks)
        g_gu = from_dp(g_gu)
        g_qkv = from_dp(g_qkv).astype(F32)
        g_do = g_do.transpose(1, 0, 2).reshape(-1, width).astype(F32)
        total_down, total_out = g_do[:-rows], g_do[-rows:]
        total_gate = g_gu[:, 0].reshape(rows, -1).astype(F32)
        total_up = g_gu[:, 1].reshape(rows, -1).astype(F32)
        each = rows // n_dp
        total_query, total_key, total_value = (
            g_qkv[:, m * each : (m + 1) * each].reshape(rows, width) for m in range(3)
        )
    else:

        def total(g):
            g = lax.psum_scatter(g.astype(F32), KEY, scatter_dimension=0, tiled=True)
            return lax.psum(g.astype(BF16), "dp").astype(F32)

        wide = lambda g: g.transpose(1, 0, 2).reshape(g.shape[1], width)
        total_query, total_key, total_value = (
            total(g_qkv[0][0, 0, m * width : (m + 1) * width]) for m in range(3)
        )
        total_gate, total_up = total(g_gu[0, 0, 0, 0]), total(g_gu[0, 0, 0, 1])
        total_down, total_out = total(wide(g_do[0][:, :ff])), total(wide(g_do[0][:, ff:]))

    def of_gain(gain, *pairs):
        terms = sum(jnp.sum(w.astype(F32) * g, axis=1) for w, g in pairs)
        return terms / gain.astype(F32)

    total_attn = of_gain(
        attn_gain, (query_proj, total_query), (key_proj, total_key), (value_proj, total_value)
    )
    total_ffn = of_gain(ffn_gain, (gate_proj, total_gate), (up_proj, total_up))
    return (
        outputs[None],
        input_grad[None],
        total_query,
        total_key,
        total_value,
        total_out,
        total_gate,
        total_up,
        total_down,
        total_attn,
        total_ffn,
        new_keys,
        new_values,
    )


def solution(mesh):
    n_dp, n_key = mesh.shape["dp"], mesh.shape["key"]
    plan = Plan(n_dp, n_key)
    fine = jax.sharding.Mesh(mesh.devices.reshape(n_dp, n_key // 2, 2), ("dp",) + KEY)
    rows, cache = P(("dp",) + KEY, None, None), P("dp", KEY, None)
    weight, gain = P(KEY, None), P(KEY)
    return jax.shard_map(
        functools.partial(per_device, plan),
        mesh=fine,
        in_specs=(rows, P(("dp",) + KEY, None), P("dp"), P("dp"), cache, cache)
        + (weight,) * 7
        + (gain, gain, rows),
        out_specs=(rows, rows) + (weight,) * 7 + (gain, gain, cache, cache),
        check_vma=False,
    )
```

```python
import functools
import math

import jax
import jax.numpy as jnp
from jax import lax
from jax.experimental import pallas as pl
from jax.experimental.pallas import tpu as pltpu
from jax.sharding import PartitionSpec as P

H = 8
HD = 128
EPSILON = 1e-05
ROPE_BASE = 10000.0
NEG_FILL = -1e30
SCALE = 1.0 / math.sqrt(HD)
BF16 = jnp.bfloat16
F32 = jnp.float32
COLS = 256
GAIN_ROWS = 16
KEY = ("z", "core")
VMEM_LIMIT = 58 * 1024 * 1024


def dot(left, right):
    return jnp.dot(left, right, preferred_element_type=F32)


def dot_nt(left, right):
    return lax.dot_general(left, right, (((1,), (1,)), ((), ())), preferred_element_type=F32)


def dot_tn(left, right):
    return lax.dot_general(left, right, (((0,), (0,)), ((), ())), preferred_element_type=F32)


def inverse_rms(values):
    return lax.rsqrt(jnp.mean(values * values, axis=-1, keepdims=True) + EPSILON)


def turn(values, cosine, sine):
    return values * cosine + pltpu.roll(values, HD // 2, 1) * sine


def cost(flops):
    return pl.CostEstimate(flops=flops, bytes_accessed=24 * 2**20, transcendentals=0)


class Plan:
    def __init__(self, n_dp, n_key):
        self.n_dp, self.n_key = n_dp, n_key
        self.fast = n_dp == 4 and n_key == 8
        self.halves = 2 if self.fast else 1


def swap(values, axis, size, distance):
    return lax.ppermute(values, axis, [(i, i ^ distance) for i in range(size)])


def own_quarter(weight, n_dp):
    width = weight.shape[1] // n_dp
    return lax.dynamic_slice_in_dim(weight, lax.axis_index("dp") * width, width, 1)


def along_z(quarter):
    return [quarter] + [swap(quarter, KEY, 8, 2 * r) for r in (1, 2, 3)]


def across_first(held):
    return [held, swap(held, "dp", 4, 1), swap(held, "dp", 4, 2)]


def across_second(near):
    return near + [swap(near[1][:2], "dp", 4, 2), swap(near[2][2:], "dp", 4, 1)]


def other_core(pieces):
    return [swap(piece, KEY, 8, 1) for piece in pieces]


def after(values, token):
    return lax.optimization_barrier((values, token))[0]


def place(plan, pieces, first_row, rows, target, sem):
    copies = []
    q, key = lax.axis_index("dp"), lax.axis_index(KEY)
    for core in range(2):
        own, x, y, far_low, far_high = pieces[core * 5 : core * 5 + 5]
        for far in range(4):
            for zr in range(4):
                if far < 3:
                    source = (own, x, y)[far].at[zr]
                else:
                    source = far_low.at[zr] if zr < 2 else far_high.at[zr - 2]
                row = pl.multiple_of((key ^ (2 * zr + core)) * rows, 16)
                column = pl.multiple_of((q ^ far) * COLS, COLS)
                copies.append(
                    pltpu.make_async_copy(
                        source.at[pl.ds(first_row, rows)],
                        target.at[pl.ds(row, rows), pl.ds(column, COLS)],
                        sem,
                    )
                )
    return copies


def place_rows(plan, held, target, sem):
    z = lax.axis_index("z")
    rows = held.shape[3]
    return [
        pltpu.make_async_copy(
            held.at[far, core, zr],
            target.at[
                pl.ds(pl.multiple_of((((z ^ zr) * 2 + core) * 4 + far) * rows, 16), rows)
            ],
            sem,
        )
        for core in range(2)
        for far in range(4)
        for zr in range(4)
    ]


def slot(far, zr):
    half = zr // 2
    return half, ((0, 1, 2, 3), (0, 2, 1, 3))[half][far], zr % 2


def store_turned(plan, values, flat, target, relative):
    if not plan.fast:
        target[...] = values.T.reshape(target.shape)
        return
    flat[...] = values.T
    q, key = lax.axis_index("dp"), lax.axis_index(KEY)
    z = lax.axis_index("z")
    rows = flat.shape[0] // 32
    for core in range(2):
        for far in range(4):
            for zr in range(4):
                if relative:
                    block = (key ^ (2 * zr + core)) * 4 + (q ^ far)
                    half, pos, low = slot(far, zr)
                    row = ((half * 4 + pos) * 2 + low) * rows
                    place_at = (core, slice(row, row + rows))
                else:
                    block = ((z ^ zr) * 2 + core) * 4 + far
                    row = ((far * 2 + core) * 4 + zr) * rows
                    place_at = slice(row, row + rows)
                target[place_at] = flat[pl.ds(pl.multiple_of(block * rows, rows), rows), :]


def project_kernel(plan, n_pieces, x_ref, cos_ref, sin_ref, *refs):
    pieces, refs = refs[:n_pieces], refs[n_pieces:]
    qmem_ref, qloc_ref, kloc_ref, kraw_ref, v_ref, normed_ref, gains_ref, w_ref, g_ref, sems = refs
    width = x_ref.shape[1]
    if plan.fast:
        rows = width // plan.n_key
        copies = []
        for m in range(3):
            copies += place(plan, pieces, GAIN_ROWS + m * rows, rows, w_ref.at[m], sems.at[0])
        key = lax.axis_index(KEY)
        for core in range(2):
            for zr in range(4):
                copies.append(
                    pltpu.make_async_copy(
                        pieces[core * 5].at[zr, pl.ds(0, GAIN_ROWS)],
                        g_ref.at[key ^ (2 * zr + core)],
                        sems.at[1],
                    )
                )
        for copy in copies:
            copy.start()
        pltpu.make_async_copy(g_ref, g_ref, sems.at[1]).wait()
        lead = [g_ref[k][0:1, :].astype(F32) for k in range(plan.n_key)]
        attn_gain = jnp.concatenate([row[:, :rows] for row in lead], axis=1)
        ffn_gain = jnp.concatenate([row[:, rows:] for row in lead], axis=1)
    else:
        copy = pltpu.make_async_copy(pieces[0], w_ref, sems.at[0])
        copy.start()
        attn_gain = pieces[1][0:1, :]
        ffn_gain = pieces[1][1:2, :]
    gains_ref[0:1, :] = attn_gain
    gains_ref[1:2, :] = ffn_gain
    x = x_ref[...].astype(F32)
    normed = (x * inverse_rms(x) * attn_gain).astype(BF16)
    normed_ref[...] = normed
    pltpu.make_async_copy(w_ref, w_ref, sems.at[0]).wait()
    cosine, sine = cos_ref[...], sin_ref[...]
    for m in range(3):
        for c in range(width // COLS):
            cols = slice(c * COLS, (c + 1) * COLS)
            raw = dot(normed, w_ref[m, :, cols])
            low = raw.astype(BF16)
            if m == 2:
                v_ref[:, cols] = low
                continue
            (qmem_ref if m == 0 else kraw_ref)[:, cols] = low
            out = qloc_ref if m == 0 else kloc_ref
            for h in range(COLS // HD):
                part = raw[:, h * HD : (h + 1) * HD]
                start = c * COLS + h * HD
                out[:, start : start + HD] = turn(part, cosine, sine).astype(BF16)


def project(plan, x, cosine, sine, pieces):
    tokens, width = x.shape
    whole = pl.BlockSpec(memory_space=pltpu.VMEM)
    anywhere = pl.BlockSpec(memory_space=pl.ANY)
    row = jax.ShapeDtypeStruct((tokens, width), BF16)
    return pl.pallas_call(
        functools.partial(project_kernel, plan, len(pieces)),
        out_shape=[row] * 6 + [jax.ShapeDtypeStruct((2, width), F32)],
        in_specs=[whole] * 3 + ([anywhere] * len(pieces) if plan.fast else [anywhere, whole]),
        out_specs=[whole] * 7,
        scratch_shapes=[
            pltpu.VMEM((3, width, width), BF16),
            pltpu.VMEM((plan.n_key, GAIN_ROWS, COLS), BF16),
            pltpu.SemaphoreType.DMA((2,)),
        ],
        compiler_params=pltpu.CompilerParams(vmem_limit_bytes=VMEM_LIMIT),
        cost_estimate=cost(6 * tokens * width * width),
        name="project",
    )(x, cosine, sine, *pieces)


def flat_rows(ref):
    block = ref[...]
    return block.reshape(block.shape[0] * block.shape[1], block.shape[2])


def weigh_kernel(qmem, qloc, kloc, mem_k, local_bias, memory_bias, p_loc, p_mem):
    s_loc = dot_nt(qloc[...], kloc[...]) * SCALE + local_bias[...]
    s_mem = dot_nt(qmem[...], flat_rows(mem_k)) * SCALE + memory_bias[...]
    largest = jnp.maximum(
        jnp.max(s_loc, axis=-1, keepdims=True), jnp.max(s_mem, axis=-1, keepdims=True)
    )
    e_loc = jnp.exp(s_loc - largest)
    e_mem = jnp.exp(s_mem - largest)
    total = jnp.sum(e_loc, axis=-1, keepdims=True) + jnp.sum(e_mem, axis=-1, keepdims=True)
    inverse = 1.0 / total
    p_loc[0] = (e_loc * inverse).astype(BF16)
    p_mem[0] = (e_mem * inverse).astype(BF16)


def head_spec(tokens):
    return pl.BlockSpec((tokens, HD), lambda h: (0, h))


def memory_spec(memory):
    return pl.BlockSpec(memory.shape[:2] + (HD,), lambda h: (0, 0, h))


def prob_specs(tokens, keys):
    return [
        pl.BlockSpec((1, tokens, tokens), lambda h: (h, 0, 0)),
        pl.BlockSpec((1, tokens, keys), lambda h: (h, 0, 0)),
    ]


def weigh(qmem, qloc, kloc, mem_k, local_bias, memory_bias):
    tokens, width = qmem.shape
    keys = memory_bias.shape[1]
    return pl.pallas_call(
        weigh_kernel,
        grid=(width // HD,),
        in_specs=[head_spec(tokens)] * 3
        + [
            memory_spec(mem_k),
            pl.BlockSpec((tokens, tokens), lambda h: (0, 0)),
            pl.BlockSpec((1, keys), lambda h: (0, 0)),
        ],
        out_specs=prob_specs(tokens, keys),
        out_shape=[
            jax.ShapeDtypeStruct((width // HD, tokens, tokens), BF16),
            jax.ShapeDtypeStruct((width // HD, tokens, keys), BF16),
        ],
        compiler_params=pltpu.CompilerParams(vmem_limit_bytes=VMEM_LIMIT),
        cost_estimate=cost(4 * tokens * (tokens + keys) * width),
        name="weigh",
    )(qmem, qloc, kloc, mem_k, local_bias, memory_bias)


def attend_kernel(p_loc, p_mem, v, mem_v, out):
    out[...] = (dot(p_loc[0], v[...]) + dot(p_mem[0], flat_rows(mem_v))).astype(BF16)


def attend(p_loc, p_mem, v, mem_v):
    tokens, width = v.shape
    keys = p_mem.shape[2]
    return pl.pallas_call(
        attend_kernel,
        grid=(width // HD,),
        in_specs=prob_specs(tokens, keys) + [head_spec(tokens), memory_spec(mem_v)],
        out_specs=head_spec(tokens),
        out_shape=jax.ShapeDtypeStruct((tokens, width), BF16),
        compiler_params=pltpu.CompilerParams(vmem_limit_bytes=VMEM_LIMIT),
        cost_estimate=cost(2 * tokens * (tokens + keys) * width),
        name="attend",
    )(p_loc, p_mem, v, mem_v)


def feed_kernel(plan, n_pieces, x_ref, att_ref, ct_ref, gains_ref, *refs):
    pieces, refs = refs[:n_pieces], refs[n_pieces:]
    n_half = plan.halves
    gu_ref, do_refs, refs = refs[0], refs[1 : 1 + n_half], refs[1 + n_half :]
    out_ref, dmix_ref, datt_ref = refs[:3]
    wo, wd, wgu, mixed, normed, flat, turned, acc_out, acc_back, g_down, g_out, sems = refs[3:]
    step = pl.program_id(0)
    tokens, width = x_ref.shape
    ff = wd.shape[0]
    gain = gains_ref[1:2, :]

    @pl.when(step == 0)
    def _():
        if plan.fast:
            rows = width // plan.n_key
            copies = place(plan, pieces, 0, rows, wo, sems.at[0])
            copies += place_rows(plan, pieces[-1], wgu, sems.at[1])
            copies += place(plan, pieces, rows, ff // plan.n_key, wd, sems.at[2])
        else:
            copies = [
                pltpu.make_async_copy(piece, held, sems.at[i])
                for i, (piece, held) in enumerate(zip(pieces, (wo, wgu, wd)))
            ]
        for copy in copies:
            copy.start()
        pltpu.make_async_copy(wo, wo, sems.at[0]).wait()
        mixed[...] = x_ref[...].astype(F32) + dot(att_ref[...], wo[...])
        value = mixed[...]
        low = (value * inverse_rms(value) * gain).astype(BF16)
        normed[...] = low
        store_turned(plan, low, flat, turned, False)
        acc_out[...] = jnp.zeros_like(acc_out)
        acc_back[...] = jnp.zeros_like(acc_back)
        pltpu.make_async_copy(wgu, wgu, sems.at[1]).wait()
        pltpu.make_async_copy(wd, wd, sems.at[2]).wait()

    ct = ct_ref[...]
    first = pl.multiple_of(step * COLS, COLS)
    down = wd[pl.ds(first, COLS), :]
    w_gate = wgu[:, pl.ds(first, COLS)]
    w_up = wgu[:, pl.ds(first + ff, COLS)]
    gate = dot(normed[...], w_gate)
    up = dot(normed[...], w_up)
    back = dot_nt(ct, down)
    sigma = 1.0 / (1.0 + jnp.exp(-gate))
    swish = gate * sigma
    hidden = (swish * up).astype(BF16)
    d_gate = (back * up * (sigma * (1.0 + gate * (1.0 - sigma)))).astype(BF16)
    d_up = (back * swish).astype(BF16)
    acc_out[...] += dot(hidden, down)
    acc_back[...] += dot_nt(d_gate, w_gate) + dot_nt(d_up, w_up)
    grad_down = dot_tn(hidden, ct).astype(BF16)
    for c in range(width // COLS):
        g_down[c, pl.ds(first, COLS), :] = grad_down[:, c * COLS : (c + 1) * COLS]
    lead = gu_ref.shape[:3]
    for i, grad in enumerate((d_gate, d_up)):
        value = dot(turned[...], grad).astype(BF16)
        gu_ref[:, :, :, i] = value.reshape(lead + (-1, COLS))

    @pl.when(step == pl.num_programs(0) - 1)
    def _():
        copies = []

        def send(source, offset):
            if not plan.fast:
                n = source.shape[1]
                for c in range(width // COLS):
                    copies.append(
                        pltpu.make_async_copy(
                            source.at[c], do_refs[0].at[c, pl.ds(offset, n)], sems.at[0]
                        )
                    )
            else:
                q, key = lax.axis_index("dp"), lax.axis_index(KEY)
                n = source.shape[1] // plan.n_key
                for core in range(2):
                    for far in range(4):
                        for zr in range(4):
                            row = pl.multiple_of((key ^ (2 * zr + core)) * n, 16)
                            copies.append(
                                pltpu.make_async_copy(
                                    source.at[q ^ far, pl.ds(row, n)],
                                    do_refs[core].at[slot(far, zr)].at[pl.ds(offset, n)],
                                    sems.at[0],
                                )
                            )

        send(g_down, 0)
        for copy in copies:
            copy.start()
        value = mixed[...]
        out_ref[...] = (value + acc_out[...]).astype(BF16)
        rf = inverse_rms(value)
        d_normed = acc_back[...]
        scaled = d_normed * gain
        d_mixed = (
            ct.astype(F32)
            + rf * scaled
            - value * (rf * rf * rf) * jnp.mean(scaled * value, axis=-1, keepdims=True)
        )
        dmix_ref[...] = d_mixed
        branch = d_mixed.astype(BF16)
        for c in range(width // COLS):
            g_out[c] = dot_tn(att_ref[...], branch[:, c * COLS : (c + 1) * COLS]).astype(BF16)
        started = len(copies)
        send(g_out, (ff if not plan.fast else ff // plan.n_key))
        for copy in copies[started:]:
            copy.start()
        datt_ref[...] = dot_nt(branch, wo[...]).astype(BF16)
        for copy in copies:
            copy.wait()


def feed(plan, x, attended, ct, gains, pieces, ff):
    tokens, width = x.shape
    steps = ff // COLS
    const = lambda *block: pl.BlockSpec(block, lambda j: (0,) * len(block))
    anywhere = pl.BlockSpec(memory_space=pl.ANY)
    if plan.fast:
        lead = (plan.n_dp, 2, plan.n_key // 2)
        rows = width // (plan.n_dp * plan.n_key)
        do_shape = (2, 4, 2, (ff + width) // plan.n_key, COLS)
    else:
        lead, rows = (1, 1, 1), width
        do_shape = (width // COLS, ff + width, COLS)
    return pl.pallas_call(
        functools.partial(feed_kernel, plan, len(pieces)),
        grid=(steps,),
        in_specs=[const(tokens, width)] * 3 + [const(2, width)] + [anywhere] * len(pieces),
        out_specs=[pl.BlockSpec(lead + (2, rows, COLS), lambda j: (0, 0, 0, 0, 0, j))]
        + [anywhere] * plan.halves
        + [const(tokens, width)] * 3,
        out_shape=[jax.ShapeDtypeStruct(lead + (2, rows, ff), BF16)]
        + [jax.ShapeDtypeStruct(do_shape, BF16)] * plan.halves
        + [
            jax.ShapeDtypeStruct((tokens, width), BF16),
            jax.ShapeDtypeStruct((tokens, width), F32),
            jax.ShapeDtypeStruct((tokens, width), BF16),
        ],
        scratch_shapes=[
            pltpu.VMEM((width, width), BF16),
            pltpu.VMEM((ff, width), BF16),
            pltpu.VMEM((width, 2 * ff), BF16),
            pltpu.VMEM((tokens, width), F32),
            pltpu.VMEM((tokens, width), BF16),
            pltpu.VMEM((width, tokens), BF16),
            pltpu.VMEM((width, tokens), BF16),
            pltpu.VMEM((tokens, width), F32),
            pltpu.VMEM((tokens, width), F32),
            pltpu.VMEM((width // COLS, ff, COLS), BF16),
            pltpu.VMEM((width // COLS, width, COLS), BF16),
            pltpu.SemaphoreType.DMA((3,)),
        ],
        compiler_params=pltpu.CompilerParams(vmem_limit_bytes=VMEM_LIMIT),
        cost_estimate=cost(18 * tokens * width * ff),
        name="feed",
    )(x, attended, ct, gains, *pieces)


def attend_back_kernel(
    p_loc, p_mem, datt, att, qloc, kloc, v, mem_k, mem_v, cos_ref, sin_ref, dq_ref, dk_ref, dv_ref
):
    grad = datt[...]
    delta = jnp.sum(grad.astype(F32) * att[...].astype(F32), axis=-1, keepdims=True)
    low_loc = p_loc[0]
    ds_loc = (low_loc.astype(F32) * (dot_nt(grad, v[...]) - delta)).astype(BF16)
    ds_mem = (p_mem[0].astype(F32) * (dot_nt(grad, flat_rows(mem_v)) - delta)).astype(BF16)
    cosine, sine = cos_ref[...], sin_ref[...]
    dq_loc = dot(ds_loc, kloc[...]) * SCALE
    dq_mem = dot(ds_mem, flat_rows(mem_k)) * SCALE
    dk = dot_tn(ds_loc, qloc[...]) * SCALE
    dq_ref[...] = (dq_mem + turn(dq_loc, cosine, -sine)).astype(BF16)
    dk_ref[...] = turn(dk, cosine, -sine).astype(BF16)
    dv_ref[...] = dot_tn(low_loc, grad).astype(BF16)


def attend_back(p_loc, p_mem, datt, att, qloc, kloc, v, mem_k, mem_v, cosine, sine):
    tokens, width = datt.shape
    keys = p_mem.shape[2]
    table = pl.BlockSpec((tokens, HD), lambda h: (0, 0))
    return pl.pallas_call(
        attend_back_kernel,
        grid=(width // HD,),
        in_specs=prob_specs(tokens, keys)
        + [head_spec(tokens)] * 5
        + [memory_spec(mem_k), memory_spec(mem_v), table, table],
        out_specs=[head_spec(tokens)] * 3,
        out_shape=[jax.ShapeDtypeStruct((tokens, width), BF16)] * 3,
        compiler_params=pltpu.CompilerParams(vmem_limit_bytes=VMEM_LIMIT),
        cost_estimate=cost(4 * tokens * (2 * tokens + keys) * width),
        name="attend_back",
    )(p_loc, p_mem, datt, att, qloc, kloc, v, mem_k, mem_v, cosine, sine)


def project_grads_kernel(plan, normed_ref, dq, dk, dv, *refs):
    n_half = plan.halves
    g_refs, (flat, turned) = refs[:n_half], refs[n_half:]
    width = normed_ref.shape[1]
    store_turned(plan, normed_ref[...], flat, turned, True)
    low = (dq, dk, dv)
    for half in range(n_half):
        each = g_refs[half].shape[-2] // 3
        lead = g_refs[half].shape[:-2]
        for m in range(3):
            for c in range(width // COLS):
                cols = slice(c * COLS, (c + 1) * COLS)
                value = dot(turned[half], low[m][:, cols]).astype(BF16)
                g_refs[half][..., m * each : (m + 1) * each, cols] = value.reshape(
                    lead + (each, COLS)
                )


def project_grads(plan, normed, dq, dk, dv):
    tokens, width = normed.shape
    whole = pl.BlockSpec(memory_space=pltpu.VMEM)
    if plan.fast:
        lead, rows = (2, 4, 2), width // (plan.n_dp * plan.n_key)
    else:
        lead, rows = (1, 1), width
    return pl.pallas_call(
        functools.partial(project_grads_kernel, plan),
        in_specs=[whole] * 4,
        out_specs=[whole] * plan.halves,
        out_shape=[jax.ShapeDtypeStruct(lead + (3 * rows, width), BF16)] * plan.halves,
        scratch_shapes=[
            pltpu.VMEM((width, tokens), BF16),
            pltpu.VMEM((plan.halves, width // plan.halves, tokens), BF16),
        ],
        compiler_params=pltpu.CompilerParams(vmem_limit_bytes=VMEM_LIMIT),
        cost_estimate=cost(2**20),
        name="project_grads",
    )(normed, dq, dk, dv)


def project_back_kernel(plan, n_pieces, x_ref, dmix_ref, gains_ref, dq, dk, dv, *refs):
    pieces, refs = refs[:n_pieces], refs[n_pieces:]
    xgrad_ref, w_ref, sems = refs
    if plan.fast:
        rows = x_ref.shape[1] // plan.n_key
        for m in range(3):
            for copy in place(plan, pieces, GAIN_ROWS + m * rows, rows, w_ref.at[m], sems.at[0]):
                copy.start()
    else:
        pltpu.make_async_copy(pieces[0], w_ref, sems.at[0]).start()
    x = x_ref[...].astype(F32)
    ra = inverse_rms(x)
    pltpu.make_async_copy(w_ref, w_ref, sems.at[0]).wait()
    d_normed = dot_nt(dq[...], w_ref[0]) + dot_nt(dk[...], w_ref[1]) + dot_nt(dv[...], w_ref[2])
    scaled = d_normed * gains_ref[0:1, :]
    xgrad_ref[...] = (
        dmix_ref[...]
        + ra * scaled
        - x * (ra * ra * ra) * jnp.mean(scaled * x, axis=-1, keepdims=True)
    )


def project_back(plan, x, dmix, gains, dq, dk, dv, pieces):
    tokens, width = x.shape
    whole = pl.BlockSpec(memory_space=pltpu.VMEM)
    return pl.pallas_call(
        functools.partial(project_back_kernel, plan, len(pieces)),
        in_specs=[whole] * 6 + [pl.BlockSpec(memory_space=pl.ANY)] * len(pieces),
        out_specs=whole,
        out_shape=jax.ShapeDtypeStruct((tokens, width), F32),
        scratch_shapes=[pltpu.VMEM((3, width, width), BF16), pltpu.SemaphoreType.DMA((1,))],
        compiler_params=pltpu.CompilerParams(vmem_limit_bytes=VMEM_LIMIT),
        cost_estimate=cost(2**20),
        name="project_back",
    )(x, dmix, gains, dq, dk, dv, *pieces)


def add(*parts):
    total = parts[0].astype(F32)
    for part in parts[1:]:
        total = total + part.astype(F32)
    return total.astype(BF16)


def both_cores(own, other):
    return add(own, swap(other, KEY, 8, 1))


def over_dp_first(share, token=None):
    from_y = swap(share[0, 2:], "dp", 4, 2)
    from_x = swap(share[1, 2:], "dp", 4, 1)
    if token is not None:
        from_y, from_x = after((from_y, from_x), token)
    mine = share[0, 0], from_y[0], share[1, 0], from_x[0]
    return mine, (add(share[0, 1], from_y[1]), add(share[1, 1], from_x[1]))


def over_dp_second(mine, passed, token):
    low, high = swap(passed[0], "dp", 4, 1), swap(passed[1], "dp", 4, 2)
    low, high = after((low, high), token)
    low, high = add(*mine[:2], low), add(*mine[2:], high)
    return [low[0], low[1], high[0], high[1]]


def over_z(parts, token=None):
    come = [swap(parts[r], KEY, 8, 2 * r) for r in (1, 2, 3)]
    if token is not None:
        come = after(come, token)
    return add(parts[0], *come)


def from_dp(share, token=None):
    held = [share] + [swap(share, "dp", 4, r) for r in (1, 2, 3)]
    if token is not None:
        held = after(held, token)
    held = jnp.stack(held)
    return jnp.take(held, jnp.arange(4) ^ lax.axis_index("dp"), axis=0)


def per_device(
    plan,
    inputs,
    positions,
    memory_flag,
    partner,
    cache_keys,
    cache_values,
    query_proj,
    key_proj,
    value_proj,
    out_proj,
    gate_proj,
    up_proj,
    down_proj,
    attn_gain,
    ffn_gain,
    cotangent,
):
    x, ct, token_pos = inputs[0], cotangent[0], positions[0]
    tokens, width = x.shape
    group, slots = cache_keys.shape[0], cache_keys.shape[1]
    key = lax.axis_index(KEY)
    n_dp = plan.n_dp

    half = HD // 2
    frequency = ROPE_BASE ** (-2.0 * jnp.arange(half, dtype=F32) / HD)
    angles = token_pos.astype(F32)[:, None] * frequency[None, :]
    cosine, sine = jnp.cos(angles), jnp.sin(angles)
    cosine = jnp.concatenate([cosine, cosine], axis=1)
    sine = jnp.concatenate([-sine, sine], axis=1)
    order = jnp.arange(tokens, dtype=jnp.int32)
    valid = (order[None, :] <= order[:, None]) & (
        token_pos[:, None] - token_pos[None, :] == order[:, None] - order[None, :]
    )
    local_bias = jnp.where(valid, 0.0, NEG_FILL).astype(F32)
    self_flag = jnp.take(memory_flag, key)
    place_in_slot = jnp.arange(group * 2 * slots, dtype=jnp.int32) % (2 * slots)
    memory_bias = jnp.where((place_in_slot >= slots) | (self_flag == 1), 0.0, NEG_FILL)
    memory_bias = memory_bias.astype(F32)[None, :]

    out_k, out_v = (
        jnp.concatenate([cache, jnp.take(cache, partner, axis=0)], axis=1)
        for cache in (cache_keys, cache_values)
    )
    rows = width // plan.n_key
    if plan.fast:
        gains = jnp.concatenate([attn_gain, ffn_gain])[None, :]
        project_in = jnp.concatenate(
            [jnp.broadcast_to(gains, (GAIN_ROWS, COLS))]
            + [own_quarter(w, n_dp) for w in (query_proj, key_proj, value_proj)],
            axis=0,
        )
        project_out = jnp.concatenate([own_quarter(w, n_dp) for w in (out_proj, down_proj)], axis=0)
        share = rows // n_dp
        gate_up = jnp.concatenate(
            [
                lax.dynamic_slice_in_dim(w, lax.axis_index("dp") * share, share, 0)
                for w in (gate_proj, up_proj)
            ],
            axis=1,
        )
        gate_up = along_z(gate_up)
        gate_up = after(gate_up, (project_in, project_out, out_k, out_v))
        project_in = along_z(after(project_in, gate_up))
        project_out = along_z(after(project_out, project_in))
        out_k = after(out_k, project_out)
        gate_up = lax.all_gather(jnp.stack(gate_up), ("dp", "core"), axis=0, tiled=False)
        gate_up = gate_up.reshape((n_dp, 2) + gate_up.shape[1:])
        project_in = across_second(across_first(jnp.stack(project_in)))
        project_out = across_first(jnp.stack(after(project_out, project_in)))
        out_v = after(out_v, project_in)
        first = project_in + other_core(project_in)
    else:
        whole = lambda w: lax.all_gather(w, KEY, axis=0, tiled=True)
        first = [
            jnp.stack([whole(query_proj), whole(key_proj), whole(value_proj)]),
            jnp.stack([whole(attn_gain), whole(ffn_gain)]).astype(F32),
        ]
        second = [
            whole(out_proj),
            whole(jnp.concatenate([gate_proj, up_proj], axis=1)),
            whole(down_proj),
        ]
    mem_k = lax.all_to_all(out_k, KEY, split_axis=0, concat_axis=0, tiled=True)
    out_v = after(out_v, mem_k)
    mem_v = lax.all_to_all(out_v, KEY, split_axis=0, concat_axis=0, tiled=True)

    qmem, qloc, kloc, kraw, v, normed, gains = project(plan, x, cosine, sine, first)
    p_loc, p_mem = weigh(qmem, qloc, kloc, mem_k, local_bias, memory_bias)
    if plan.fast:
        project_out = across_second(after(project_out, p_loc))
        second = project_out + other_core(project_out) + [gate_up]
    attended = attend(p_loc, p_mem, v, mem_v)

    run = tokens // group
    fresh = jnp.stack([kraw.reshape(group, run, width), v.reshape(group, run, width)], axis=1)
    fresh = after(fresh, attended)
    arrived = lax.all_to_all(fresh, KEY, split_axis=0, concat_axis=0, tiled=True)
    new_keys = jnp.concatenate([cache_keys[:, run:], arrived[:, 0]], axis=1)
    new_values = jnp.concatenate([cache_values[:, run:], arrived[:, 1]], axis=1)

    n_half, ff = plan.halves, gate_proj.shape[1]
    results = feed(plan, x, attended, ct, gains, second, ff)
    g_gu, g_do, (outputs, dmix, datt) = (
        results[0],
        results[1 : 1 + n_half],
        results[1 + n_half :],
    )
    if plan.fast:
        g_gu = g_gu.reshape((8,) + g_gu.shape[2:])
        g_gu = lax.psum_scatter(g_gu, ("dp", "core"), scatter_dimension=0, tiled=True)
        g_gu = lax.optimization_barrier(g_gu)
    if plan.fast:
        g_do = both_cores(*g_do)
        datt = after(datt, g_do)
    dq, dk, dv = attend_back(
        p_loc, p_mem, datt, attended, qloc, kloc, v, mem_k, mem_v, cosine, sine
    )
    if plan.fast:
        do_mine, do_passed = over_dp_first(g_do, dq)
        dq = after(dq, do_passed)
    g_qkv = project_grads(plan, normed, dq, dk, dv)
    dq = after(dq, g_qkv)
    if plan.fast:
        do_blocks = over_dp_second(do_mine, do_passed, g_qkv)
        dq = after(dq, do_blocks)
    input_grad = project_back(
        plan, x, dmix, gains, dq, dk, dv, first if plan.fast else first[:1]
    )

    if plan.fast:
        own, swapped = g_qkv[0], swap(g_qkv[1], KEY, 8, 1)
        g_qkv = add(*after((own, swapped), (input_grad, arrived)))
        g_do = over_z(do_blocks, g_qkv)
        g_gu = after(g_gu, g_do)[0]
        mine, passed = over_dp_first(g_qkv, g_gu)
        g_gu = over_z(g_gu, passed)
        blocks = over_dp_second(mine, passed, g_gu)
        g_do = from_dp(g_do, blocks)
        g_qkv = over_z(blocks)
        g_gu = from_dp(g_gu, g_qkv)
        g_qkv = from_dp(g_qkv).astype(F32)
        g_do = g_do.transpose(1, 0, 2).reshape(-1, width).astype(F32)
        total_down, total_out = g_do[:-rows], g_do[-rows:]
        total_gate = g_gu[:, 0].reshape(rows, -1).astype(F32)
        total_up = g_gu[:, 1].reshape(rows, -1).astype(F32)
        each = rows // n_dp
        total_query, total_key, total_value = (
            g_qkv[:, m * each : (m + 1) * each].reshape(rows, width) for m in range(3)
        )
    else:

        def total(g):
            g = lax.psum_scatter(g.astype(F32), KEY, scatter_dimension=0, tiled=True)
            return lax.psum(g.astype(BF16), "dp").astype(F32)

        wide = lambda g: g.transpose(1, 0, 2).reshape(g.shape[1], width)
        total_query, total_key, total_value = (
            total(g_qkv[0][0, 0, m * width : (m + 1) * width]) for m in range(3)
        )
        total_gate, total_up = total(g_gu[0, 0, 0, 0]), total(g_gu[0, 0, 0, 1])
        total_down, total_out = total(wide(g_do[0][:, :ff])), total(wide(g_do[0][:, ff:]))

    def of_gain(gain, *pairs):
        terms = sum(jnp.sum(w.astype(F32) * g, axis=1) for w, g in pairs)
        return terms / gain.astype(F32)

    total_attn = of_gain(
        attn_gain, (query_proj, total_query), (key_proj, total_key), (value_proj, total_value)
    )
    total_ffn = of_gain(ffn_gain, (gate_proj, total_gate), (up_proj, total_up))
    return (
        outputs[None],
        input_grad[None],
        total_query,
        total_key,
        total_value,
        total_out,
        total_gate,
        total_up,
        total_down,
        total_attn,
        total_ffn,
        new_keys,
        new_values,
    )


def solution(mesh):
    n_dp, n_key = mesh.shape["dp"], mesh.shape["key"]
    plan = Plan(n_dp, n_key)
    fine = jax.sharding.Mesh(mesh.devices.reshape(n_dp, n_key // 2, 2), ("dp",) + KEY)
    rows, cache = P(("dp",) + KEY, None, None), P("dp", KEY, None)
    weight, gain = P(KEY, None), P(KEY)
    return jax.shard_map(
        functools.partial(per_device, plan),
        mesh=fine,
        in_specs=(rows, P(("dp",) + KEY, None), P("dp"), P("dp"), cache, cache)
        + (weight,) * 7
        + (gain, gain, rows),
        out_specs=(rows, rows) + (weight,) * 7 + (gain, gain, cache, cache),
        check_vma=False,
    )
```

```python
import functools
import math

import jax
import jax.numpy as jnp
from jax import lax
from jax.experimental import pallas as pl
from jax.experimental.pallas import tpu as pltpu
from jax.sharding import PartitionSpec as P

H = 8
HD = 128
EPSILON = 1e-05
ROPE_BASE = 10000.0
NEG_FILL = -1e30
SCALE = 1.0 / math.sqrt(HD)
BF16 = jnp.bfloat16
F32 = jnp.float32
COLS = 256
GAIN_ROWS = 16
KEY = ("z", "core")
VMEM_LIMIT = 58 * 1024 * 1024


def dot(left, right):
    return jnp.dot(left, right, preferred_element_type=F32)


def dot_nt(left, right):
    return lax.dot_general(left, right, (((1,), (1,)), ((), ())), preferred_element_type=F32)


def dot_tn(left, right):
    return lax.dot_general(left, right, (((0,), (0,)), ((), ())), preferred_element_type=F32)


def inverse_rms(values):
    return lax.rsqrt(jnp.mean(values * values, axis=-1, keepdims=True) + EPSILON)


def turn(values, cosine, sine):
    return values * cosine + pltpu.roll(values, HD // 2, 1) * sine


def cost(flops):
    return pl.CostEstimate(flops=flops, bytes_accessed=24 * 2**20, transcendentals=0)


class Plan:
    def __init__(self, n_dp, n_key):
        self.n_dp, self.n_key = n_dp, n_key
        self.fast = n_dp == 4 and n_key == 8
        self.halves = 2 if self.fast else 1


def swap(values, axis, size, distance):
    return lax.ppermute(values, axis, [(i, i ^ distance) for i in range(size)])


def own_quarter(weight, n_dp):
    width = weight.shape[1] // n_dp
    return lax.dynamic_slice_in_dim(weight, lax.axis_index("dp") * width, width, 1)


def along_z(quarter):
    return [quarter] + [swap(quarter, KEY, 8, 2 * r) for r in (1, 2, 3)]


def across_first(held):
    return [held, swap(held, "dp", 4, 1), swap(held, "dp", 4, 2)]


def across_second(near):
    return near + [swap(near[1][:2], "dp", 4, 2), swap(near[2][2:], "dp", 4, 1)]


def other_core(pieces):
    return [swap(piece, KEY, 8, 1) for piece in pieces]


def after(values, token):
    return lax.optimization_barrier((values, token))[0]


def place(plan, pieces, first_row, rows, target, sem):
    copies = []
    q, key = lax.axis_index("dp"), lax.axis_index(KEY)
    for core in range(2):
        own, x, y, far_low, far_high = pieces[core * 5 : core * 5 + 5]
        for far in range(4):
            for zr in range(4):
                if far < 3:
                    source = (own, x, y)[far].at[zr]
                else:
                    source = far_low.at[zr] if zr < 2 else far_high.at[zr - 2]
                row = pl.multiple_of((key ^ (2 * zr + core)) * rows, 16)
                column = pl.multiple_of((q ^ far) * COLS, COLS)
                copies.append(
                    pltpu.make_async_copy(
                        source.at[pl.ds(first_row, rows)],
                        target.at[pl.ds(row, rows), pl.ds(column, COLS)],
                        sem,
                    )
                )
    return copies


def place_rows(plan, held, target, sem):
    z = lax.axis_index("z")
    rows = held.shape[3]
    return [
        pltpu.make_async_copy(
            held.at[far, core, zr],
            target.at[
                pl.ds(pl.multiple_of((((z ^ zr) * 2 + core) * 4 + far) * rows, 16), rows)
            ],
            sem,
        )
        for core in range(2)
        for far in range(4)
        for zr in range(4)
    ]


def slot(far, zr):
    half = zr // 2
    return half, ((0, 1, 2, 3), (0, 2, 1, 3))[half][far], zr % 2


def store_turned(plan, values, flat, target, relative):
    if not plan.fast:
        target[...] = values.T.reshape(target.shape)
        return
    flat[...] = values.T
    q, key = lax.axis_index("dp"), lax.axis_index(KEY)
    z = lax.axis_index("z")
    rows = flat.shape[0] // 32
    for core in range(2):
        for far in range(4):
            for zr in range(4):
                if relative:
                    block = (key ^ (2 * zr + core)) * 4 + (q ^ far)
                    half, pos, low = slot(far, zr)
                    row = ((half * 4 + pos) * 2 + low) * rows
                    place_at = (core, slice(row, row + rows))
                else:
                    block = ((z ^ zr) * 2 + core) * 4 + far
                    row = ((far * 2 + core) * 4 + zr) * rows
                    place_at = slice(row, row + rows)
                target[place_at] = flat[pl.ds(pl.multiple_of(block * rows, rows), rows), :]


def project_kernel(plan, n_pieces, x_ref, cos_ref, sin_ref, *refs):
    pieces, refs = refs[:n_pieces], refs[n_pieces:]
    qmem_ref, qloc_ref, kloc_ref, kraw_ref, v_ref, normed_ref, gains_ref, w_ref, g_ref, sems = refs
    width = x_ref.shape[1]
    if plan.fast:
        rows = width // plan.n_key
        copies = []
        for m in range(3):
            copies += place(plan, pieces, GAIN_ROWS + m * rows, rows, w_ref.at[m], sems.at[0])
        key = lax.axis_index(KEY)
        for core in range(2):
            for zr in range(4):
                copies.append(
                    pltpu.make_async_copy(
                        pieces[core * 5].at[zr, pl.ds(0, GAIN_ROWS)],
                        g_ref.at[key ^ (2 * zr + core)],
                        sems.at[1],
                    )
                )
        for copy in copies:
            copy.start()
        pltpu.make_async_copy(g_ref, g_ref, sems.at[1]).wait()
        lead = [g_ref[k][0:1, :].astype(F32) for k in range(plan.n_key)]
        attn_gain = jnp.concatenate([row[:, :rows] for row in lead], axis=1)
        ffn_gain = jnp.concatenate([row[:, rows:] for row in lead], axis=1)
    else:
        copy = pltpu.make_async_copy(pieces[0], w_ref, sems.at[0])
        copy.start()
        attn_gain = pieces[1][0:1, :]
        ffn_gain = pieces[1][1:2, :]
    gains_ref[0:1, :] = attn_gain
    gains_ref[1:2, :] = ffn_gain
    x = x_ref[...].astype(F32)
    normed = (x * inverse_rms(x) * attn_gain).astype(BF16)
    normed_ref[...] = normed
    pltpu.make_async_copy(w_ref, w_ref, sems.at[0]).wait()
    cosine, sine = cos_ref[...], sin_ref[...]
    for m in range(3):
        for c in range(width // COLS):
            cols = slice(c * COLS, (c + 1) * COLS)
            raw = dot(normed, w_ref[m, :, cols])
            low = raw.astype(BF16)
            if m == 2:
                v_ref[:, cols] = low
                continue
            (qmem_ref if m == 0 else kraw_ref)[:, cols] = low
            out = qloc_ref if m == 0 else kloc_ref
            for h in range(COLS // HD):
                part = raw[:, h * HD : (h + 1) * HD]
                start = c * COLS + h * HD
                out[:, start : start + HD] = turn(part, cosine, sine).astype(BF16)


def project(plan, x, cosine, sine, pieces):
    tokens, width = x.shape
    whole = pl.BlockSpec(memory_space=pltpu.VMEM)
    anywhere = pl.BlockSpec(memory_space=pl.ANY)
    row = jax.ShapeDtypeStruct((tokens, width), BF16)
    return pl.pallas_call(
        functools.partial(project_kernel, plan, len(pieces)),
        out_shape=[row] * 6 + [jax.ShapeDtypeStruct((2, width), F32)],
        in_specs=[whole] * 3 + ([anywhere] * len(pieces) if plan.fast else [anywhere, whole]),
        out_specs=[whole] * 7,
        scratch_shapes=[
            pltpu.VMEM((3, width, width), BF16),
            pltpu.VMEM((plan.n_key, GAIN_ROWS, COLS), BF16),
            pltpu.SemaphoreType.DMA((2,)),
        ],
        compiler_params=pltpu.CompilerParams(vmem_limit_bytes=VMEM_LIMIT),
        cost_estimate=cost(6 * tokens * width * width),
        name="project",
    )(x, cosine, sine, *pieces)


def flat_rows(ref):
    block = ref[...]
    return block.reshape(block.shape[0] * block.shape[1], block.shape[2])


def weigh_kernel(qmem, qloc, kloc, mem_k, local_bias, memory_bias, p_loc, p_mem):
    s_loc = dot_nt(qloc[...], kloc[...]) * SCALE + local_bias[...]
    s_mem = dot_nt(qmem[...], flat_rows(mem_k)) * SCALE + memory_bias[...]
    largest = jnp.maximum(
        jnp.max(s_loc, axis=-1, keepdims=True), jnp.max(s_mem, axis=-1, keepdims=True)
    )
    e_loc = jnp.exp(s_loc - largest)
    e_mem = jnp.exp(s_mem - largest)
    total = jnp.sum(e_loc, axis=-1, keepdims=True) + jnp.sum(e_mem, axis=-1, keepdims=True)
    inverse = 1.0 / total
    p_loc[0] = (e_loc * inverse).astype(BF16)
    p_mem[0] = (e_mem * inverse).astype(BF16)


def head_spec(tokens, heads=1):
    return pl.BlockSpec((tokens, heads * HD), lambda h: (0, h))


def memory_spec(memory, heads=1):
    return pl.BlockSpec(memory.shape[:2] + (heads * HD,), lambda h: (0, 0, h))


def prob_specs(tokens, keys, heads=1):
    return [
        pl.BlockSpec((heads, tokens, tokens), lambda h: (h, 0, 0)),
        pl.BlockSpec((heads, tokens, keys), lambda h: (h, 0, 0)),
    ]


def weigh(qmem, qloc, kloc, mem_k, local_bias, memory_bias):
    tokens, width = qmem.shape
    keys = memory_bias.shape[1]
    return pl.pallas_call(
        weigh_kernel,
        grid=(width // HD,),
        in_specs=[head_spec(tokens)] * 3
        + [
            memory_spec(mem_k),
            pl.BlockSpec((tokens, tokens), lambda h: (0, 0)),
            pl.BlockSpec((1, keys), lambda h: (0, 0)),
        ],
        out_specs=prob_specs(tokens, keys),
        out_shape=[
            jax.ShapeDtypeStruct((width // HD, tokens, tokens), BF16),
            jax.ShapeDtypeStruct((width // HD, tokens, keys), BF16),
        ],
        compiler_params=pltpu.CompilerParams(vmem_limit_bytes=VMEM_LIMIT),
        cost_estimate=cost(4 * tokens * (tokens + keys) * width),
        name="weigh",
    )(qmem, qloc, kloc, mem_k, local_bias, memory_bias)


def attend_kernel(p_loc, p_mem, v, mem_v, out):
    values = flat_rows(mem_v)
    for i in range(2):
        cols = slice(i * HD, (i + 1) * HD)
        out[:, cols] = (dot(p_loc[i], v[:, cols]) + dot(p_mem[i], values[:, cols])).astype(BF16)


def attend(p_loc, p_mem, v, mem_v):
    tokens, width = v.shape
    keys = p_mem.shape[2]
    return pl.pallas_call(
        attend_kernel,
        grid=(width // HD // 2,),
        in_specs=prob_specs(tokens, keys, 2) + [head_spec(tokens, 2), memory_spec(mem_v, 2)],
        out_specs=head_spec(tokens, 2),
        out_shape=jax.ShapeDtypeStruct((tokens, width), BF16),
        compiler_params=pltpu.CompilerParams(vmem_limit_bytes=VMEM_LIMIT),
        cost_estimate=cost(2 * tokens * (tokens + keys) * width),
        name="attend",
    )(p_loc, p_mem, v, mem_v)


def feed_kernel(plan, n_pieces, x_ref, att_ref, ct_ref, gains_ref, *refs):
    pieces, refs = refs[:n_pieces], refs[n_pieces:]
    n_half = plan.halves
    gu_ref, do_refs, refs = refs[0], refs[1 : 1 + n_half], refs[1 + n_half :]
    out_ref, dmix_ref, datt_ref = refs[:3]
    wo, wd, wgu, mixed, normed, flat, turned, acc_out, acc_back, g_down, g_out, sems = refs[3:]
    step = pl.program_id(0)
    tokens, width = x_ref.shape
    ff = wd.shape[0]
    gain = gains_ref[1:2, :]

    @pl.when(step == 0)
    def _():
        if plan.fast:
            rows = width // plan.n_key
            copies = place(plan, pieces, 0, rows, wo, sems.at[0])
            copies += place_rows(plan, pieces[-1], wgu, sems.at[1])
            copies += place(plan, pieces, rows, ff // plan.n_key, wd, sems.at[2])
        else:
            copies = [
                pltpu.make_async_copy(piece, held, sems.at[i])
                for i, (piece, held) in enumerate(zip(pieces, (wo, wgu, wd)))
            ]
        for copy in copies:
            copy.start()
        pltpu.make_async_copy(wo, wo, sems.at[0]).wait()
        mixed[...] = x_ref[...].astype(F32) + dot(att_ref[...], wo[...])
        value = mixed[...]
        low = (value * inverse_rms(value) * gain).astype(BF16)
        normed[...] = low
        store_turned(plan, low, flat, turned, False)
        acc_out[...] = jnp.zeros_like(acc_out)
        acc_back[...] = jnp.zeros_like(acc_back)
        pltpu.make_async_copy(wgu, wgu, sems.at[1]).wait()
        pltpu.make_async_copy(wd, wd, sems.at[2]).wait()

    ct = ct_ref[...]
    first = pl.multiple_of(step * COLS, COLS)
    down = wd[pl.ds(first, COLS), :]
    w_gate = wgu[:, pl.ds(first, COLS)]
    w_up = wgu[:, pl.ds(first + ff, COLS)]
    gate = dot(normed[...], w_gate)
    up = dot(normed[...], w_up)
    back = dot_nt(ct, down)
    sigma = 0.5 + 0.5 * jnp.tanh(0.5 * gate)
    swish = gate * sigma
    hidden = (swish * up).astype(BF16)
    d_gate = (back * up * (sigma * (1.0 + gate * (1.0 - sigma)))).astype(BF16)
    d_up = (back * swish).astype(BF16)
    acc_out[...] += dot(hidden, down)
    acc_back[...] += dot_nt(d_gate, w_gate) + dot_nt(d_up, w_up)
    grad_down = dot_tn(hidden, ct).astype(BF16)
    for c in range(width // COLS):
        g_down[c, pl.ds(first, COLS), :] = grad_down[:, c * COLS : (c + 1) * COLS]
    lead = gu_ref.shape[:3]
    for i, grad in enumerate((d_gate, d_up)):
        value = dot(turned[...], grad).astype(BF16)
        gu_ref[:, :, :, i] = value.reshape(lead + (-1, COLS))

    @pl.when(step == pl.num_programs(0) - 1)
    def _():
        copies = []

        def send(source, offset):
            if not plan.fast:
                n = source.shape[1]
                for c in range(width // COLS):
                    copies.append(
                        pltpu.make_async_copy(
                            source.at[c], do_refs[0].at[c, pl.ds(offset, n)], sems.at[0]
                        )
                    )
            else:
                q, key = lax.axis_index("dp"), lax.axis_index(KEY)
                n = source.shape[1] // plan.n_key
                for core in range(2):
                    for far in range(4):
                        for zr in range(4):
                            row = pl.multiple_of((key ^ (2 * zr + core)) * n, 16)
                            copies.append(
                                pltpu.make_async_copy(
                                    source.at[q ^ far, pl.ds(row, n)],
                                    do_refs[core].at[slot(far, zr)].at[pl.ds(offset, n)],
                                    sems.at[0],
                                )
                            )

        send(g_down, 0)
        for copy in copies:
            copy.start()
        value = mixed[...]
        out_ref[...] = (value + acc_out[...]).astype(BF16)
        rf = inverse_rms(value)
        d_normed = acc_back[...]
        scaled = d_normed * gain
        d_mixed = (
            ct.astype(F32)
            + rf * scaled
            - value * (rf * rf * rf) * jnp.mean(scaled * value, axis=-1, keepdims=True)
        )
        dmix_ref[...] = d_mixed
        branch = d_mixed.astype(BF16)
        for c in range(width // COLS):
            g_out[c] = dot_tn(att_ref[...], branch[:, c * COLS : (c + 1) * COLS]).astype(BF16)
        started = len(copies)
        send(g_out, (ff if not plan.fast else ff // plan.n_key))
        for copy in copies[started:]:
            copy.start()
        datt_ref[...] = dot_nt(branch, wo[...]).astype(BF16)
        for copy in copies:
            copy.wait()


def feed(plan, x, attended, ct, gains, pieces, ff):
    tokens, width = x.shape
    steps = ff // COLS
    const = lambda *block: pl.BlockSpec(block, lambda j: (0,) * len(block))
    anywhere = pl.BlockSpec(memory_space=pl.ANY)
    if plan.fast:
        lead = (plan.n_dp, 2, plan.n_key // 2)
        rows = width // (plan.n_dp * plan.n_key)
        do_shape = (2, 4, 2, (ff + width) // plan.n_key, COLS)
    else:
        lead, rows = (1, 1, 1), width
        do_shape = (width // COLS, ff + width, COLS)
    return pl.pallas_call(
        functools.partial(feed_kernel, plan, len(pieces)),
        grid=(steps,),
        in_specs=[const(tokens, width)] * 3 + [const(2, width)] + [anywhere] * len(pieces),
        out_specs=[pl.BlockSpec(lead + (2, rows, COLS), lambda j: (0, 0, 0, 0, 0, j))]
        + [anywhere] * plan.halves
        + [const(tokens, width)] * 3,
        out_shape=[jax.ShapeDtypeStruct(lead + (2, rows, ff), BF16)]
        + [jax.ShapeDtypeStruct(do_shape, BF16)] * plan.halves
        + [
            jax.ShapeDtypeStruct((tokens, width), BF16),
            jax.ShapeDtypeStruct((tokens, width), F32),
            jax.ShapeDtypeStruct((tokens, width), BF16),
        ],
        scratch_shapes=[
            pltpu.VMEM((width, width), BF16),
            pltpu.VMEM((ff, width), BF16),
            pltpu.VMEM((width, 2 * ff), BF16),
            pltpu.VMEM((tokens, width), F32),
            pltpu.VMEM((tokens, width), BF16),
            pltpu.VMEM((width, tokens), BF16),
            pltpu.VMEM((width, tokens), BF16),
            pltpu.VMEM((tokens, width), F32),
            pltpu.VMEM((tokens, width), F32),
            pltpu.VMEM((width // COLS, ff, COLS), BF16),
            pltpu.VMEM((width // COLS, width, COLS), BF16),
            pltpu.SemaphoreType.DMA((3,)),
        ],
        compiler_params=pltpu.CompilerParams(vmem_limit_bytes=VMEM_LIMIT),
        cost_estimate=cost(18 * tokens * width * ff),
        name="feed",
    )(x, attended, ct, gains, *pieces)


def attend_back_kernel(
    p_loc, p_mem, datt, att, qloc, kloc, v, mem_k, mem_v, cos_ref, sin_ref, dq_ref, dk_ref, dv_ref
):
    keys, values = flat_rows(mem_k), flat_rows(mem_v)
    cosine, sine = cos_ref[...], sin_ref[...]
    for i in range(2):
        cols = slice(i * HD, (i + 1) * HD)
        grad, k_loc = datt[:, cols], kloc[:, cols]
        delta = jnp.sum(grad.astype(F32) * att[:, cols].astype(F32), axis=-1, keepdims=True)
        low_loc = p_loc[i]
        ds_loc = (low_loc.astype(F32) * (dot_nt(grad, v[:, cols]) - delta)).astype(BF16)
        ds_mem = (p_mem[i].astype(F32) * (dot_nt(grad, values[:, cols]) - delta)).astype(BF16)
        dq_loc = dot(ds_loc, k_loc) * SCALE
        dq_mem = dot(ds_mem, keys[:, cols]) * SCALE
        dk = dot_tn(ds_loc, qloc[:, cols]) * SCALE
        dq_ref[:, cols] = (dq_mem + turn(dq_loc, cosine, -sine)).astype(BF16)
        dk_ref[:, cols] = turn(dk, cosine, -sine).astype(BF16)
        dv_ref[:, cols] = dot_tn(low_loc, grad).astype(BF16)


def attend_back(p_loc, p_mem, datt, att, qloc, kloc, v, mem_k, mem_v, cosine, sine):
    tokens, width = datt.shape
    keys = p_mem.shape[2]
    table = pl.BlockSpec((tokens, HD), lambda h: (0, 0))
    return pl.pallas_call(
        attend_back_kernel,
        grid=(width // HD // 2,),
        in_specs=prob_specs(tokens, keys, 2)
        + [head_spec(tokens, 2)] * 5
        + [memory_spec(mem_k, 2), memory_spec(mem_v, 2), table, table],
        out_specs=[head_spec(tokens, 2)] * 3,
        out_shape=[jax.ShapeDtypeStruct((tokens, width), BF16)] * 3,
        compiler_params=pltpu.CompilerParams(vmem_limit_bytes=VMEM_LIMIT),
        cost_estimate=cost(4 * tokens * (2 * tokens + keys) * width),
        name="attend_back",
    )(p_loc, p_mem, datt, att, qloc, kloc, v, mem_k, mem_v, cosine, sine)


def project_grads_kernel(plan, normed_ref, dq, dk, dv, *refs):
    n_half = plan.halves
    g_refs, (flat, turned) = refs[:n_half], refs[n_half:]
    width = normed_ref.shape[1]
    store_turned(plan, normed_ref[...], flat, turned, True)
    low = (dq, dk, dv)
    for half in range(n_half):
        each = g_refs[half].shape[-2] // 3
        lead = g_refs[half].shape[:-2]
        for m in range(3):
            for c in range(width // COLS):
                cols = slice(c * COLS, (c + 1) * COLS)
                value = dot(turned[half], low[m][:, cols]).astype(BF16)
                g_refs[half][..., m * each : (m + 1) * each, cols] = value.reshape(
                    lead + (each, COLS)
                )


def project_grads(plan, normed, dq, dk, dv):
    tokens, width = normed.shape
    whole = pl.BlockSpec(memory_space=pltpu.VMEM)
    if plan.fast:
        lead, rows = (2, 4, 2), width // (plan.n_dp * plan.n_key)
    else:
        lead, rows = (1, 1), width
    return pl.pallas_call(
        functools.partial(project_grads_kernel, plan),
        in_specs=[whole] * 4,
        out_specs=[whole] * plan.halves,
        out_shape=[jax.ShapeDtypeStruct(lead + (3 * rows, width), BF16)] * plan.halves,
        scratch_shapes=[
            pltpu.VMEM((width, tokens), BF16),
            pltpu.VMEM((plan.halves, width // plan.halves, tokens), BF16),
        ],
        compiler_params=pltpu.CompilerParams(vmem_limit_bytes=VMEM_LIMIT),
        cost_estimate=cost(2**20),
        name="project_grads",
    )(normed, dq, dk, dv)


def project_back_kernel(plan, n_pieces, x_ref, dmix_ref, gains_ref, dq, dk, dv, *refs):
    pieces, refs = refs[:n_pieces], refs[n_pieces:]
    xgrad_ref, w_ref, sems = refs
    if plan.fast:
        rows = x_ref.shape[1] // plan.n_key
        for m in range(3):
            for copy in place(plan, pieces, GAIN_ROWS + m * rows, rows, w_ref.at[m], sems.at[0]):
                copy.start()
    else:
        pltpu.make_async_copy(pieces[0], w_ref, sems.at[0]).start()
    x = x_ref[...].astype(F32)
    ra = inverse_rms(x)
    pltpu.make_async_copy(w_ref, w_ref, sems.at[0]).wait()
    d_normed = dot_nt(dq[...], w_ref[0]) + dot_nt(dk[...], w_ref[1]) + dot_nt(dv[...], w_ref[2])
    scaled = d_normed * gains_ref[0:1, :]
    xgrad_ref[...] = (
        dmix_ref[...]
        + ra * scaled
        - x * (ra * ra * ra) * jnp.mean(scaled * x, axis=-1, keepdims=True)
    )


def project_back(plan, x, dmix, gains, dq, dk, dv, pieces):
    tokens, width = x.shape
    whole = pl.BlockSpec(memory_space=pltpu.VMEM)
    return pl.pallas_call(
        functools.partial(project_back_kernel, plan, len(pieces)),
        in_specs=[whole] * 6 + [pl.BlockSpec(memory_space=pl.ANY)] * len(pieces),
        out_specs=whole,
        out_shape=jax.ShapeDtypeStruct((tokens, width), F32),
        scratch_shapes=[pltpu.VMEM((3, width, width), BF16), pltpu.SemaphoreType.DMA((1,))],
        compiler_params=pltpu.CompilerParams(vmem_limit_bytes=VMEM_LIMIT),
        cost_estimate=cost(2**20),
        name="project_back",
    )(x, dmix, gains, dq, dk, dv, *pieces)


def add(*parts):
    total = parts[0].astype(F32)
    for part in parts[1:]:
        total = total + part.astype(F32)
    return total.astype(BF16)


def both_cores(own, other):
    return add(own, swap(other, KEY, 8, 1))


def over_dp_first(share, token=None):
    from_y = swap(share[0, 2:], "dp", 4, 2)
    from_x = swap(share[1, 2:], "dp", 4, 1)
    if token is not None:
        from_y, from_x = after((from_y, from_x), token)
    mine = share[0, 0], from_y[0], share[1, 0], from_x[0]
    return mine, (add(share[0, 1], from_y[1]), add(share[1, 1], from_x[1]))


def over_dp_second(mine, passed, token):
    low, high = swap(passed[0], "dp", 4, 1), swap(passed[1], "dp", 4, 2)
    low, high = after((low, high), token)
    low, high = add(*mine[:2], low), add(*mine[2:], high)
    return [low[0], low[1], high[0], high[1]]


def over_z(parts, token=None):
    come = [swap(parts[r], KEY, 8, 2 * r) for r in (1, 2, 3)]
    if token is not None:
        come = after(come, token)
    return add(parts[0], *come)


def from_dp(share, token=None):
    held = [share] + [swap(share, "dp", 4, r) for r in (1, 2, 3)]
    if token is not None:
        held = after(held, token)
    held = jnp.stack(held)
    return jnp.take(held, jnp.arange(4) ^ lax.axis_index("dp"), axis=0)


def per_device(
    plan,
    inputs,
    positions,
    memory_flag,
    partner,
    cache_keys,
    cache_values,
    query_proj,
    key_proj,
    value_proj,
    out_proj,
    gate_proj,
    up_proj,
    down_proj,
    attn_gain,
    ffn_gain,
    cotangent,
):
    x, ct, token_pos = inputs[0], cotangent[0], positions[0]
    tokens, width = x.shape
    group, slots = cache_keys.shape[0], cache_keys.shape[1]
    key = lax.axis_index(KEY)
    n_dp = plan.n_dp

    half = HD // 2
    frequency = ROPE_BASE ** (-2.0 * jnp.arange(half, dtype=F32) / HD)
    angles = token_pos.astype(F32)[:, None] * frequency[None, :]
    cosine, sine = jnp.cos(angles), jnp.sin(angles)
    cosine = jnp.concatenate([cosine, cosine], axis=1)
    sine = jnp.concatenate([-sine, sine], axis=1)
    order = jnp.arange(tokens, dtype=jnp.int32)
    valid = (order[None, :] <= order[:, None]) & (
        token_pos[:, None] - token_pos[None, :] == order[:, None] - order[None, :]
    )
    local_bias = jnp.where(valid, 0.0, NEG_FILL).astype(F32)
    self_flag = jnp.take(memory_flag, key)
    place_in_slot = jnp.arange(group * 2 * slots, dtype=jnp.int32) % (2 * slots)
    memory_bias = jnp.where((place_in_slot >= slots) | (self_flag == 1), 0.0, NEG_FILL)
    memory_bias = memory_bias.astype(F32)[None, :]

    out_k, out_v = (
        jnp.concatenate([cache, jnp.take(cache, partner, axis=0)], axis=1)
        for cache in (cache_keys, cache_values)
    )
    rows = width // plan.n_key
    if plan.fast:
        gains = jnp.concatenate([attn_gain, ffn_gain])[None, :]
        project_in = jnp.concatenate(
            [jnp.broadcast_to(gains, (GAIN_ROWS, COLS))]
            + [own_quarter(w, n_dp) for w in (query_proj, key_proj, value_proj)],
            axis=0,
        )
        project_out = jnp.concatenate([own_quarter(w, n_dp) for w in (out_proj, down_proj)], axis=0)
        share = rows // n_dp
        gate_up = jnp.concatenate(
            [
                lax.dynamic_slice_in_dim(w, lax.axis_index("dp") * share, share, 0)
                for w in (gate_proj, up_proj)
            ],
            axis=1,
        )
        gate_up = along_z(gate_up)
        gate_up = after(gate_up, (project_in, project_out, out_k, out_v))
        project_in = along_z(after(project_in, gate_up))
        project_out = along_z(after(project_out, project_in))
        out_k = after(out_k, project_out)
        gate_up = lax.all_gather(jnp.stack(gate_up), ("dp", "core"), axis=0, tiled=False)
        gate_up = gate_up.reshape((n_dp, 2) + gate_up.shape[1:])
        project_in = across_second(across_first(jnp.stack(project_in)))
        project_out = across_first(jnp.stack(after(project_out, project_in)))
        out_v = after(out_v, project_in)
        first = project_in + other_core(project_in)
    else:
        whole = lambda w: lax.all_gather(w, KEY, axis=0, tiled=True)
        first = [
            jnp.stack([whole(query_proj), whole(key_proj), whole(value_proj)]),
            jnp.stack([whole(attn_gain), whole(ffn_gain)]).astype(F32),
        ]
        second = [
            whole(out_proj),
            whole(jnp.concatenate([gate_proj, up_proj], axis=1)),
            whole(down_proj),
        ]
    mem_k = lax.all_to_all(out_k, KEY, split_axis=0, concat_axis=0, tiled=True)
    out_v = after(out_v, mem_k)
    mem_v = lax.all_to_all(out_v, KEY, split_axis=0, concat_axis=0, tiled=True)

    qmem, qloc, kloc, kraw, v, normed, gains = project(plan, x, cosine, sine, first)
    p_loc, p_mem = weigh(qmem, qloc, kloc, mem_k, local_bias, memory_bias)
    if plan.fast:
        project_out = across_second(after(project_out, p_loc))
        p_mem = after(p_mem, project_out)
        second = project_out + other_core(project_out) + [gate_up]
    attended = attend(p_loc, p_mem, v, mem_v)

    run = tokens // group
    fresh = jnp.stack([kraw.reshape(group, run, width), v.reshape(group, run, width)], axis=1)
    fresh = after(fresh, (p_loc, project_out) if plan.fast else p_loc)
    arrived = lax.all_to_all(fresh, KEY, split_axis=0, concat_axis=0, tiled=True)
    new_keys = jnp.concatenate([cache_keys[:, run:], arrived[:, 0]], axis=1)
    new_values = jnp.concatenate([cache_values[:, run:], arrived[:, 1]], axis=1)

    n_half, ff = plan.halves, gate_proj.shape[1]
    results = feed(plan, x, attended, ct, gains, second, ff)
    g_gu, g_do, (outputs, dmix, datt) = (
        results[0],
        results[1 : 1 + n_half],
        results[1 + n_half :],
    )
    if plan.fast:
        g_gu, g_do = after((g_gu, g_do), arrived)
        g_gu = g_gu.reshape((8,) + g_gu.shape[2:])
        g_gu = lax.psum_scatter(g_gu, ("dp", "core"), scatter_dimension=0, tiled=True)
        g_gu = lax.optimization_barrier(g_gu)
    if plan.fast:
        g_do = both_cores(*g_do)
        datt = after(datt, g_do)
    dq, dk, dv = attend_back(
        p_loc, p_mem, datt, attended, qloc, kloc, v, mem_k, mem_v, cosine, sine
    )
    if plan.fast:
        do_mine, do_passed = over_dp_first(g_do, dq)
        dq = after(dq, do_passed)
    g_qkv = project_grads(plan, normed, dq, dk, dv)
    dq = after(dq, g_qkv)
    if plan.fast:
        do_blocks = over_dp_second(do_mine, do_passed, g_qkv)
        dq = after(dq, do_blocks)
    input_grad = project_back(
        plan, x, dmix, gains, dq, dk, dv, first if plan.fast else first[:1]
    )

    if plan.fast:
        own, swapped = g_qkv[0], swap(g_qkv[1], KEY, 8, 1)
        g_qkv = add(*after((own, swapped), (input_grad, arrived)))
        g_do = over_z(do_blocks, g_qkv)
        g_gu = after(g_gu, g_do)[0]
        mine, passed = over_dp_first(g_qkv, g_gu)
        g_gu = over_z(g_gu, passed)
        blocks = over_dp_second(mine, passed, g_gu)
        g_do = from_dp(g_do, blocks)
        g_qkv = over_z(blocks)
        g_gu = from_dp(g_gu, g_qkv)
        g_qkv = from_dp(g_qkv).astype(F32)
        g_do = g_do.transpose(1, 0, 2).reshape(-1, width).astype(F32)
        total_down, total_out = g_do[:-rows], g_do[-rows:]
        total_gate = g_gu[:, 0].reshape(rows, -1).astype(F32)
        total_up = g_gu[:, 1].reshape(rows, -1).astype(F32)
        each = rows // n_dp
        total_query, total_key, total_value = (
            g_qkv[:, m * each : (m + 1) * each].reshape(rows, width) for m in range(3)
        )
    else:

        def total(g):
            g = lax.psum_scatter(g.astype(F32), KEY, scatter_dimension=0, tiled=True)
            return lax.psum(g.astype(BF16), "dp").astype(F32)

        wide = lambda g: g.transpose(1, 0, 2).reshape(g.shape[1], width)
        total_query, total_key, total_value = (
            total(g_qkv[0][0, 0, m * width : (m + 1) * width]) for m in range(3)
        )
        total_gate, total_up = total(g_gu[0, 0, 0, 0]), total(g_gu[0, 0, 0, 1])
        total_down, total_out = total(wide(g_do[0][:, :ff])), total(wide(g_do[0][:, ff:]))

    def of_gain(gain, *pairs):
        terms = sum(jnp.sum(w.astype(F32) * g, axis=1) for w, g in pairs)
        return terms / gain.astype(F32)

    total_attn = of_gain(
        attn_gain, (query_proj, total_query), (key_proj, total_key), (value_proj, total_value)
    )
    total_ffn = of_gain(ffn_gain, (gate_proj, total_gate), (up_proj, total_up))
    return (
        outputs[None],
        input_grad[None],
        total_query,
        total_key,
        total_value,
        total_out,
        total_gate,
        total_up,
        total_down,
        total_attn,
        total_ffn,
        new_keys,
        new_values,
    )


def solution(mesh):
    n_dp, n_key = mesh.shape["dp"], mesh.shape["key"]
    plan = Plan(n_dp, n_key)
    fine = jax.sharding.Mesh(mesh.devices.reshape(n_dp, n_key // 2, 2), ("dp",) + KEY)
    rows, cache = P(("dp",) + KEY, None, None), P("dp", KEY, None)
    weight, gain = P(KEY, None), P(KEY)
    return jax.shard_map(
        functools.partial(per_device, plan),
        mesh=fine,
        in_specs=(rows, P(("dp",) + KEY, None), P("dp"), P("dp"), cache, cache)
        + (weight,) * 7
        + (gain, gain, rows),
        out_specs=(rows, rows) + (weight,) * 7 + (gain, gain, cache, cache),
        check_vma=False,
    )
```

```python
import functools
import math

import jax
import jax.numpy as jnp
from jax import lax
from jax.experimental import pallas as pl
from jax.experimental.pallas import tpu as pltpu
from jax.sharding import PartitionSpec as P

H = 8
HD = 128
EPSILON = 1e-05
ROPE_BASE = 10000.0
NEG_FILL = -1e30
SCALE = 1.0 / math.sqrt(HD)
BF16 = jnp.bfloat16
F32 = jnp.float32
COLS = 256
GAIN_ROWS = 16
KEY = ("z", "core")
VMEM_LIMIT = 58 * 1024 * 1024


def dot(left, right):
    return jnp.dot(left, right, preferred_element_type=F32)


def dot_nt(left, right):
    return lax.dot_general(left, right, (((1,), (1,)), ((), ())), preferred_element_type=F32)


def dot_tn(left, right):
    return lax.dot_general(left, right, (((0,), (0,)), ((), ())), preferred_element_type=F32)


def inverse_rms(values):
    return lax.rsqrt(jnp.mean(values * values, axis=-1, keepdims=True) + EPSILON)


def turn(values, cosine, sine):
    return values * cosine + pltpu.roll(values, HD // 2, 1) * sine


def cost(flops):
    return pl.CostEstimate(flops=flops, bytes_accessed=24 * 2**20, transcendentals=0)


class Plan:
    def __init__(self, n_dp, n_key):
        self.n_dp, self.n_key = n_dp, n_key
        self.fast = n_dp == 4 and n_key == 8
        self.halves = 2 if self.fast else 1


def swap(values, axis, size, distance):
    return lax.ppermute(values, axis, [(i, i ^ distance) for i in range(size)])


def own_quarter(weight, n_dp):
    width = weight.shape[1] // n_dp
    return lax.dynamic_slice_in_dim(weight, lax.axis_index("dp") * width, width, 1)


def along_z(quarter):
    return [quarter] + [swap(quarter, KEY, 8, 2 * r) for r in (1, 2, 3)]


def across_first(held):
    return [held, swap(held, "dp", 4, 1), swap(held, "dp", 4, 2)]


def across_second(near):
    return near + [swap(near[1][:2], "dp", 4, 2), swap(near[2][2:], "dp", 4, 1)]


def other_core(pieces):
    return [swap(piece, KEY, 8, 1) for piece in pieces]


def after(values, token):
    return lax.optimization_barrier((values, token))[0]


def place(plan, pieces, first_row, rows, target, sem):
    copies = []
    q, key = lax.axis_index("dp"), lax.axis_index(KEY)
    for core in range(2):
        own, x, y, far_low, far_high = pieces[core * 5 : core * 5 + 5]
        for far in range(4):
            for zr in range(4):
                if far < 3:
                    source = (own, x, y)[far].at[zr]
                else:
                    source = far_low.at[zr] if zr < 2 else far_high.at[zr - 2]
                row = pl.multiple_of((key ^ (2 * zr + core)) * rows, 16)
                column = pl.multiple_of((q ^ far) * COLS, COLS)
                copies.append(
                    pltpu.make_async_copy(
                        source.at[pl.ds(first_row, rows)],
                        target.at[pl.ds(row, rows), pl.ds(column, COLS)],
                        sem,
                    )
                )
    return copies


def place_rows(plan, held, target, sem):
    z = lax.axis_index("z")
    rows = held.shape[3]
    return [
        pltpu.make_async_copy(
            held.at[far, core, zr],
            target.at[
                pl.ds(pl.multiple_of((((z ^ zr) * 2 + core) * 4 + far) * rows, 16), rows)
            ],
            sem,
        )
        for core in range(2)
        for far in range(4)
        for zr in range(4)
    ]


def slot(far, zr):
    half = zr // 2
    return half, ((0, 1, 2, 3), (0, 2, 1, 3))[half][far], zr % 2


def store_turned(plan, values, flat, target, relative):
    if not plan.fast:
        target[...] = values.T.reshape(target.shape)
        return
    flat[...] = values.T
    q, key = lax.axis_index("dp"), lax.axis_index(KEY)
    z = lax.axis_index("z")
    rows = flat.shape[0] // 32
    for core in range(2):
        for far in range(4):
            for zr in range(4):
                if relative:
                    block = (key ^ (2 * zr + core)) * 4 + (q ^ far)
                    half, pos, low = slot(far, zr)
                    row = ((half * 4 + pos) * 2 + low) * rows
                    place_at = (core, slice(row, row + rows))
                else:
                    block = ((z ^ zr) * 2 + core) * 4 + far
                    row = ((far * 2 + core) * 4 + zr) * rows
                    place_at = slice(row, row + rows)
                target[place_at] = flat[pl.ds(pl.multiple_of(block * rows, rows), rows), :]


def project_kernel(plan, n_pieces, x_ref, cos_ref, sin_ref, *refs):
    pieces, refs = refs[:n_pieces], refs[n_pieces:]
    qmem_ref, qloc_ref, kloc_ref, kraw_ref, v_ref, normed_ref, gains_ref, w_ref, g_ref, sems = refs
    width = x_ref.shape[1]
    if plan.fast:
        rows = width // plan.n_key
        copies = []
        for m in range(3):
            copies += place(plan, pieces, GAIN_ROWS + m * rows, rows, w_ref.at[m], sems.at[0])
        key = lax.axis_index(KEY)
        for core in range(2):
            for zr in range(4):
                copies.append(
                    pltpu.make_async_copy(
                        pieces[core * 5].at[zr, pl.ds(0, GAIN_ROWS)],
                        g_ref.at[key ^ (2 * zr + core)],
                        sems.at[1],
                    )
                )
        for copy in copies:
            copy.start()
        pltpu.make_async_copy(g_ref, g_ref, sems.at[1]).wait()
        lead = [g_ref[k][0:1, :].astype(F32) for k in range(plan.n_key)]
        attn_gain = jnp.concatenate([row[:, :rows] for row in lead], axis=1)
        ffn_gain = jnp.concatenate([row[:, rows:] for row in lead], axis=1)
    else:
        copy = pltpu.make_async_copy(pieces[0], w_ref, sems.at[0])
        copy.start()
        attn_gain = pieces[1][0:1, :]
        ffn_gain = pieces[1][1:2, :]
    gains_ref[0:1, :] = attn_gain
    gains_ref[1:2, :] = ffn_gain
    x = x_ref[...].astype(F32)
    normed = (x * inverse_rms(x) * attn_gain).astype(BF16)
    normed_ref[...] = normed
    pltpu.make_async_copy(w_ref, w_ref, sems.at[0]).wait()
    cosine, sine = cos_ref[...], sin_ref[...]
    for m in range(3):
        for c in range(width // COLS):
            cols = slice(c * COLS, (c + 1) * COLS)
            raw = dot(normed, w_ref[m, :, cols])
            low = raw.astype(BF16)
            if m == 2:
                v_ref[:, cols] = low
                continue
            (qmem_ref if m == 0 else kraw_ref)[:, cols] = low
            out = qloc_ref if m == 0 else kloc_ref
            for h in range(COLS // HD):
                part = raw[:, h * HD : (h + 1) * HD]
                start = c * COLS + h * HD
                out[:, start : start + HD] = turn(part, cosine, sine).astype(BF16)


def project(plan, x, cosine, sine, pieces):
    tokens, width = x.shape
    whole = pl.BlockSpec(memory_space=pltpu.VMEM)
    anywhere = pl.BlockSpec(memory_space=pl.ANY)
    row = jax.ShapeDtypeStruct((tokens, width), BF16)
    return pl.pallas_call(
        functools.partial(project_kernel, plan, len(pieces)),
        out_shape=[row] * 6 + [jax.ShapeDtypeStruct((2, width), F32)],
        in_specs=[whole] * 3 + ([anywhere] * len(pieces) if plan.fast else [anywhere, whole]),
        out_specs=[whole] * 7,
        scratch_shapes=[
            pltpu.VMEM((3, width, width), BF16),
            pltpu.VMEM((plan.n_key, GAIN_ROWS, COLS), BF16),
            pltpu.SemaphoreType.DMA((2,)),
        ],
        compiler_params=pltpu.CompilerParams(vmem_limit_bytes=VMEM_LIMIT),
        cost_estimate=cost(6 * tokens * width * width),
        name="project",
    )(x, cosine, sine, *pieces)


def flat_rows(ref):
    block = ref[...]
    return block.reshape(block.shape[0] * block.shape[1], block.shape[2])


def weigh_kernel(qmem, qloc, kloc, mem_k, local_bias, memory_bias, p_loc, p_mem):
    keys = flat_rows(mem_k)
    for i in range(2):
        cols = slice(i * HD, (i + 1) * HD)
        s_loc = dot_nt(qloc[:, cols], kloc[:, cols]) * SCALE + local_bias[...]
        s_mem = dot_nt(qmem[:, cols], keys[:, cols]) * SCALE + memory_bias[...]
        largest = jnp.maximum(
            jnp.max(s_loc, axis=-1, keepdims=True), jnp.max(s_mem, axis=-1, keepdims=True)
        )
        e_loc = jnp.exp(s_loc - largest)
        e_mem = jnp.exp(s_mem - largest)
        total = jnp.sum(e_loc, axis=-1, keepdims=True) + jnp.sum(e_mem, axis=-1, keepdims=True)
        inverse = 1.0 / total
        p_loc[i] = (e_loc * inverse).astype(BF16)
        p_mem[i] = (e_mem * inverse).astype(BF16)


def head_spec(tokens, heads=1):
    return pl.BlockSpec((tokens, heads * HD), lambda h: (0, h))


def memory_spec(memory, heads=1):
    return pl.BlockSpec(memory.shape[:2] + (heads * HD,), lambda h: (0, 0, h))


def prob_specs(tokens, keys, heads=1):
    return [
        pl.BlockSpec((heads, tokens, tokens), lambda h: (h, 0, 0)),
        pl.BlockSpec((heads, tokens, keys), lambda h: (h, 0, 0)),
    ]


def weigh(qmem, qloc, kloc, mem_k, local_bias, memory_bias):
    tokens, width = qmem.shape
    keys = memory_bias.shape[1]
    return pl.pallas_call(
        weigh_kernel,
        grid=(width // HD // 2,),
        in_specs=[head_spec(tokens, 2)] * 3
        + [
            memory_spec(mem_k, 2),
            pl.BlockSpec((tokens, tokens), lambda h: (0, 0)),
            pl.BlockSpec((1, keys), lambda h: (0, 0)),
        ],
        out_specs=prob_specs(tokens, keys, 2),
        out_shape=[
            jax.ShapeDtypeStruct((width // HD, tokens, tokens), BF16),
            jax.ShapeDtypeStruct((width // HD, tokens, keys), BF16),
        ],
        compiler_params=pltpu.CompilerParams(vmem_limit_bytes=VMEM_LIMIT),
        cost_estimate=cost(4 * tokens * (tokens + keys) * width),
        name="weigh",
    )(qmem, qloc, kloc, mem_k, local_bias, memory_bias)


def attend_kernel(p_loc, p_mem, v, mem_v, out):
    values = flat_rows(mem_v)
    for i in range(4):
        cols = slice(i * HD, (i + 1) * HD)
        out[:, cols] = (dot(p_loc[i], v[:, cols]) + dot(p_mem[i], values[:, cols])).astype(BF16)


def attend(p_loc, p_mem, v, mem_v):
    tokens, width = v.shape
    keys = p_mem.shape[2]
    return pl.pallas_call(
        attend_kernel,
        grid=(width // HD // 4,),
        in_specs=prob_specs(tokens, keys, 4) + [head_spec(tokens, 4), memory_spec(mem_v, 4)],
        out_specs=head_spec(tokens, 4),
        out_shape=jax.ShapeDtypeStruct((tokens, width), BF16),
        compiler_params=pltpu.CompilerParams(vmem_limit_bytes=VMEM_LIMIT),
        cost_estimate=cost(2 * tokens * (tokens + keys) * width),
        name="attend",
    )(p_loc, p_mem, v, mem_v)


def feed_kernel(plan, n_pieces, x_ref, att_ref, ct_ref, gains_ref, *refs):
    pieces, refs = refs[:n_pieces], refs[n_pieces:]
    n_half = plan.halves
    gu_ref, do_refs, refs = refs[0], refs[1 : 1 + n_half], refs[1 + n_half :]
    out_ref, dmix_ref, datt_ref = refs[:3]
    wo, wd, wgu, mixed, normed, flat, turned, acc_out, acc_back, g_down, g_out, sems = refs[3:]
    step = pl.program_id(0)
    tokens, width = x_ref.shape
    ff = wd.shape[0]
    gain = gains_ref[1:2, :]

    @pl.when(step == 0)
    def _():
        if plan.fast:
            rows = width // plan.n_key
            copies = place(plan, pieces, 0, rows, wo, sems.at[0])
            copies += place_rows(plan, pieces[-1], wgu, sems.at[1])
            copies += place(plan, pieces, rows, ff // plan.n_key, wd, sems.at[2])
        else:
            copies = [
                pltpu.make_async_copy(piece, held, sems.at[i])
                for i, (piece, held) in enumerate(zip(pieces, (wo, wgu, wd)))
            ]
        for copy in copies:
            copy.start()
        pltpu.make_async_copy(wo, wo, sems.at[0]).wait()
        mixed[...] = x_ref[...].astype(F32) + dot(att_ref[...], wo[...])
        value = mixed[...]
        low = (value * inverse_rms(value) * gain).astype(BF16)
        normed[...] = low
        store_turned(plan, low, flat, turned, False)
        acc_out[...] = jnp.zeros_like(acc_out)
        acc_back[...] = jnp.zeros_like(acc_back)
        pltpu.make_async_copy(wgu, wgu, sems.at[1]).wait()
        pltpu.make_async_copy(wd, wd, sems.at[2]).wait()

    ct = ct_ref[...]
    first = pl.multiple_of(step * COLS, COLS)
    down = wd[pl.ds(first, COLS), :]
    w_gate = wgu[:, pl.ds(first, COLS)]
    w_up = wgu[:, pl.ds(first + ff, COLS)]
    gate = dot(normed[...], w_gate)
    up = dot(normed[...], w_up)
    back = dot_nt(ct, down)
    sigma = 0.5 + 0.5 * jnp.tanh(0.5 * gate)
    swish = gate * sigma
    hidden = (swish * up).astype(BF16)
    d_gate = (back * up * (sigma * (1.0 + gate * (1.0 - sigma)))).astype(BF16)
    d_up = (back * swish).astype(BF16)
    acc_out[...] += dot(hidden, down)
    acc_back[...] += dot_nt(d_gate, w_gate) + dot_nt(d_up, w_up)
    grad_down = dot_tn(hidden, ct).astype(BF16)
    for c in range(width // COLS):
        g_down[c, pl.ds(first, COLS), :] = grad_down[:, c * COLS : (c + 1) * COLS]
    lead = gu_ref.shape[:3]
    for i, grad in enumerate((d_gate, d_up)):
        value = dot(turned[...], grad).astype(BF16)
        gu_ref[:, :, :, i] = value.reshape(lead + (-1, COLS))

    @pl.when(step == pl.num_programs(0) - 1)
    def _():
        copies = []

        def send(source, offset):
            if not plan.fast:
                n = source.shape[1]
                for c in range(width // COLS):
                    copies.append(
                        pltpu.make_async_copy(
                            source.at[c], do_refs[0].at[c, pl.ds(offset, n)], sems.at[0]
                        )
                    )
            else:
                q, key = lax.axis_index("dp"), lax.axis_index(KEY)
                n = source.shape[1] // plan.n_key
                for core in range(2):
                    for far in range(4):
                        for zr in range(4):
                            row = pl.multiple_of((key ^ (2 * zr + core)) * n, 16)
                            copies.append(
                                pltpu.make_async_copy(
                                    source.at[q ^ far, pl.ds(row, n)],
                                    do_refs[core].at[slot(far, zr)].at[pl.ds(offset, n)],
                                    sems.at[0],
                                )
                            )

        send(g_down, 0)
        for copy in copies:
            copy.start()
        value = mixed[...]
        out_ref[...] = (value + acc_out[...]).astype(BF16)
        rf = inverse_rms(value)
        d_normed = acc_back[...]
        scaled = d_normed * gain
        d_mixed = (
            ct.astype(F32)
            + rf * scaled
            - value * (rf * rf * rf) * jnp.mean(scaled * value, axis=-1, keepdims=True)
        )
        dmix_ref[...] = d_mixed
        branch = d_mixed.astype(BF16)
        for c in range(width // COLS):
            g_out[c] = dot_tn(att_ref[...], branch[:, c * COLS : (c + 1) * COLS]).astype(BF16)
        started = len(copies)
        send(g_out, (ff if not plan.fast else ff // plan.n_key))
        for copy in copies[started:]:
            copy.start()
        datt_ref[...] = dot_nt(branch, wo[...]).astype(BF16)
        for copy in copies:
            copy.wait()


def feed(plan, x, attended, ct, gains, pieces, ff):
    tokens, width = x.shape
    steps = ff // COLS
    const = lambda *block: pl.BlockSpec(block, lambda j: (0,) * len(block))
    anywhere = pl.BlockSpec(memory_space=pl.ANY)
    if plan.fast:
        lead = (plan.n_dp, 2, plan.n_key // 2)
        rows = width // (plan.n_dp * plan.n_key)
        do_shape = (2, 4, 2, (ff + width) // plan.n_key, COLS)
    else:
        lead, rows = (1, 1, 1), width
        do_shape = (width // COLS, ff + width, COLS)
    return pl.pallas_call(
        functools.partial(feed_kernel, plan, len(pieces)),
        grid=(steps,),
        in_specs=[const(tokens, width)] * 3 + [const(2, width)] + [anywhere] * len(pieces),
        out_specs=[pl.BlockSpec(lead + (2, rows, COLS), lambda j: (0, 0, 0, 0, 0, j))]
        + [anywhere] * plan.halves
        + [const(tokens, width)] * 3,
        out_shape=[jax.ShapeDtypeStruct(lead + (2, rows, ff), BF16)]
        + [jax.ShapeDtypeStruct(do_shape, BF16)] * plan.halves
        + [
            jax.ShapeDtypeStruct((tokens, width), BF16),
            jax.ShapeDtypeStruct((tokens, width), F32),
            jax.ShapeDtypeStruct((tokens, width), BF16),
        ],
        scratch_shapes=[
            pltpu.VMEM((width, width), BF16),
            pltpu.VMEM((ff, width), BF16),
            pltpu.VMEM((width, 2 * ff), BF16),
            pltpu.VMEM((tokens, width), F32),
            pltpu.VMEM((tokens, width), BF16),
            pltpu.VMEM((width, tokens), BF16),
            pltpu.VMEM((width, tokens), BF16),
            pltpu.VMEM((tokens, width), F32),
            pltpu.VMEM((tokens, width), F32),
            pltpu.VMEM((width // COLS, ff, COLS), BF16),
            pltpu.VMEM((width // COLS, width, COLS), BF16),
            pltpu.SemaphoreType.DMA((3,)),
        ],
        compiler_params=pltpu.CompilerParams(vmem_limit_bytes=VMEM_LIMIT),
        cost_estimate=cost(18 * tokens * width * ff),
        name="feed",
    )(x, attended, ct, gains, *pieces)


def attend_back_kernel(
    p_loc, p_mem, datt, att, qloc, kloc, v, mem_k, mem_v, cos_ref, sin_ref, dq_ref, dk_ref, dv_ref
):
    keys, values = flat_rows(mem_k), flat_rows(mem_v)
    cosine, sine = cos_ref[...], sin_ref[...]
    for i in range(2):
        cols = slice(i * HD, (i + 1) * HD)
        grad, k_loc = datt[:, cols], kloc[:, cols]
        delta = jnp.sum(grad.astype(F32) * att[:, cols].astype(F32), axis=-1, keepdims=True)
        low_loc = p_loc[i]
        ds_loc = (low_loc.astype(F32) * (dot_nt(grad, v[:, cols]) - delta)).astype(BF16)
        ds_mem = (p_mem[i].astype(F32) * (dot_nt(grad, values[:, cols]) - delta)).astype(BF16)
        dq_loc = dot(ds_loc, k_loc) * SCALE
        dq_mem = dot(ds_mem, keys[:, cols]) * SCALE
        dk = dot_tn(ds_loc, qloc[:, cols]) * SCALE
        dq_ref[:, cols] = (dq_mem + turn(dq_loc, cosine, -sine)).astype(BF16)
        dk_ref[:, cols] = turn(dk, cosine, -sine).astype(BF16)
        dv_ref[:, cols] = dot_tn(low_loc, grad).astype(BF16)


def attend_back(p_loc, p_mem, datt, att, qloc, kloc, v, mem_k, mem_v, cosine, sine):
    tokens, width = datt.shape
    keys = p_mem.shape[2]
    table = pl.BlockSpec((tokens, HD), lambda h: (0, 0))
    return pl.pallas_call(
        attend_back_kernel,
        grid=(width // HD // 2,),
        in_specs=prob_specs(tokens, keys, 2)
        + [head_spec(tokens, 2)] * 5
        + [memory_spec(mem_k, 2), memory_spec(mem_v, 2), table, table],
        out_specs=[head_spec(tokens, 2)] * 3,
        out_shape=[jax.ShapeDtypeStruct((tokens, width), BF16)] * 3,
        compiler_params=pltpu.CompilerParams(vmem_limit_bytes=VMEM_LIMIT),
        cost_estimate=cost(4 * tokens * (2 * tokens + keys) * width),
        name="attend_back",
    )(p_loc, p_mem, datt, att, qloc, kloc, v, mem_k, mem_v, cosine, sine)


def project_grads_kernel(plan, normed_ref, dq, dk, dv, *refs):
    n_half = plan.halves
    g_refs, (flat, turned) = refs[:n_half], refs[n_half:]
    width = normed_ref.shape[1]
    store_turned(plan, normed_ref[...], flat, turned, True)
    low = (dq, dk, dv)
    for half in range(n_half):
        each = g_refs[half].shape[-2] // 3
        lead = g_refs[half].shape[:-2]
        for m in range(3):
            for c in range(width // COLS):
                cols = slice(c * COLS, (c + 1) * COLS)
                value = dot(turned[half], low[m][:, cols]).astype(BF16)
                g_refs[half][..., m * each : (m + 1) * each, cols] = value.reshape(
                    lead + (each, COLS)
                )


def project_grads(plan, normed, dq, dk, dv):
    tokens, width = normed.shape
    whole = pl.BlockSpec(memory_space=pltpu.VMEM)
    if plan.fast:
        lead, rows = (2, 4, 2), width // (plan.n_dp * plan.n_key)
    else:
        lead, rows = (1, 1), width
    return pl.pallas_call(
        functools.partial(project_grads_kernel, plan),
        in_specs=[whole] * 4,
        out_specs=[whole] * plan.halves,
        out_shape=[jax.ShapeDtypeStruct(lead + (3 * rows, width), BF16)] * plan.halves,
        scratch_shapes=[
            pltpu.VMEM((width, tokens), BF16),
            pltpu.VMEM((plan.halves, width // plan.halves, tokens), BF16),
        ],
        compiler_params=pltpu.CompilerParams(vmem_limit_bytes=VMEM_LIMIT),
        cost_estimate=cost(2**20),
        name="project_grads",
    )(normed, dq, dk, dv)


def project_back_kernel(plan, n_pieces, x_ref, dmix_ref, gains_ref, dq, dk, dv, *refs):
    pieces, refs = refs[:n_pieces], refs[n_pieces:]
    xgrad_ref, w_ref, sems = refs
    if plan.fast:
        rows = x_ref.shape[1] // plan.n_key
        for m in range(3):
            for copy in place(plan, pieces, GAIN_ROWS + m * rows, rows, w_ref.at[m], sems.at[0]):
                copy.start()
    else:
        pltpu.make_async_copy(pieces[0], w_ref, sems.at[0]).start()
    x = x_ref[...].astype(F32)
    ra = inverse_rms(x)
    pltpu.make_async_copy(w_ref, w_ref, sems.at[0]).wait()
    d_normed = dot_nt(dq[...], w_ref[0]) + dot_nt(dk[...], w_ref[1]) + dot_nt(dv[...], w_ref[2])
    scaled = d_normed * gains_ref[0:1, :]
    xgrad_ref[...] = (
        dmix_ref[...]
        + ra * scaled
        - x * (ra * ra * ra) * jnp.mean(scaled * x, axis=-1, keepdims=True)
    )


def project_back(plan, x, dmix, gains, dq, dk, dv, pieces):
    tokens, width = x.shape
    whole = pl.BlockSpec(memory_space=pltpu.VMEM)
    return pl.pallas_call(
        functools.partial(project_back_kernel, plan, len(pieces)),
        in_specs=[whole] * 6 + [pl.BlockSpec(memory_space=pl.ANY)] * len(pieces),
        out_specs=whole,
        out_shape=jax.ShapeDtypeStruct((tokens, width), F32),
        scratch_shapes=[pltpu.VMEM((3, width, width), BF16), pltpu.SemaphoreType.DMA((1,))],
        compiler_params=pltpu.CompilerParams(vmem_limit_bytes=VMEM_LIMIT),
        cost_estimate=cost(2**20),
        name="project_back",
    )(x, dmix, gains, dq, dk, dv, *pieces)


def add(*parts):
    total = parts[0].astype(F32)
    for part in parts[1:]:
        total = total + part.astype(F32)
    return total.astype(BF16)


def both_cores(own, other):
    return add(own, swap(other, KEY, 8, 1))


def over_dp_first(share, token=None):
    from_y = swap(share[0, 2:], "dp", 4, 2)
    from_x = swap(share[1, 2:], "dp", 4, 1)
    if token is not None:
        from_y, from_x = after((from_y, from_x), token)
    mine = share[0, 0], from_y[0], share[1, 0], from_x[0]
    return mine, (add(share[0, 1], from_y[1]), add(share[1, 1], from_x[1]))


def over_dp_second(mine, passed, token):
    low, high = swap(passed[0], "dp", 4, 1), swap(passed[1], "dp", 4, 2)
    low, high = after((low, high), token)
    low, high = add(*mine[:2], low), add(*mine[2:], high)
    return [low[0], low[1], high[0], high[1]]


def over_z(parts, token=None):
    come = [swap(parts[r], KEY, 8, 2 * r) for r in (1, 2, 3)]
    if token is not None:
        come = after(come, token)
    return add(parts[0], *come)


def from_dp(share, token=None):
    held = [share] + [swap(share, "dp", 4, r) for r in (1, 2, 3)]
    if token is not None:
        held = after(held, token)
    held = jnp.stack(held)
    return jnp.take(held, jnp.arange(4) ^ lax.axis_index("dp"), axis=0)


def per_device(
    plan,
    inputs,
    positions,
    memory_flag,
    partner,
    cache_keys,
    cache_values,
    query_proj,
    key_proj,
    value_proj,
    out_proj,
    gate_proj,
    up_proj,
    down_proj,
    attn_gain,
    ffn_gain,
    cotangent,
):
    x, ct, token_pos = inputs[0], cotangent[0], positions[0]
    tokens, width = x.shape
    group, slots = cache_keys.shape[0], cache_keys.shape[1]
    key = lax.axis_index(KEY)
    n_dp = plan.n_dp

    half = HD // 2
    frequency = ROPE_BASE ** (-2.0 * jnp.arange(half, dtype=F32) / HD)
    angles = token_pos.astype(F32)[:, None] * frequency[None, :]
    cosine, sine = jnp.cos(angles), jnp.sin(angles)
    cosine = jnp.concatenate([cosine, cosine], axis=1)
    sine = jnp.concatenate([-sine, sine], axis=1)
    order = jnp.arange(tokens, dtype=jnp.int32)
    valid = (order[None, :] <= order[:, None]) & (
        token_pos[:, None] - token_pos[None, :] == order[:, None] - order[None, :]
    )
    local_bias = jnp.where(valid, 0.0, NEG_FILL).astype(F32)
    self_flag = jnp.take(memory_flag, key)
    place_in_slot = jnp.arange(group * 2 * slots, dtype=jnp.int32) % (2 * slots)
    memory_bias = jnp.where((place_in_slot >= slots) | (self_flag == 1), 0.0, NEG_FILL)
    memory_bias = memory_bias.astype(F32)[None, :]

    out_k, out_v = (
        jnp.concatenate([cache, jnp.take(cache, partner, axis=0)], axis=1)
        for cache in (cache_keys, cache_values)
    )
    rows = width // plan.n_key
    if plan.fast:
        gains = jnp.concatenate([attn_gain, ffn_gain])[None, :]
        project_in = jnp.concatenate(
            [jnp.broadcast_to(gains, (GAIN_ROWS, COLS))]
            + [own_quarter(w, n_dp) for w in (query_proj, key_proj, value_proj)],
            axis=0,
        )
        project_out = jnp.concatenate([own_quarter(w, n_dp) for w in (out_proj, down_proj)], axis=0)
        share = rows // n_dp
        gate_up = jnp.concatenate(
            [
                lax.dynamic_slice_in_dim(w, lax.axis_index("dp") * share, share, 0)
                for w in (gate_proj, up_proj)
            ],
            axis=1,
        )
        gate_up = along_z(gate_up)
        gate_up = after(gate_up, (project_in, project_out, out_k, out_v))
        project_in = along_z(after(project_in, gate_up))
        project_out = along_z(after(project_out, project_in))
        out_k = after(out_k, project_out)
        gate_up = lax.all_gather(jnp.stack(gate_up), ("dp", "core"), axis=0, tiled=False)
        gate_up = gate_up.reshape((n_dp, 2) + gate_up.shape[1:])
        project_in = across_second(across_first(jnp.stack(project_in)))
        project_out = across_first(jnp.stack(after(project_out, project_in)))
        out_v = after(out_v, project_in)
        first = project_in + other_core(project_in)
    else:
        whole = lambda w: lax.all_gather(w, KEY, axis=0, tiled=True)
        first = [
            jnp.stack([whole(query_proj), whole(key_proj), whole(value_proj)]),
            jnp.stack([whole(attn_gain), whole(ffn_gain)]).astype(F32),
        ]
        second = [
            whole(out_proj),
            whole(jnp.concatenate([gate_proj, up_proj], axis=1)),
            whole(down_proj),
        ]
    mem_k = lax.all_to_all(out_k, KEY, split_axis=0, concat_axis=0, tiled=True)
    out_v = after(out_v, mem_k)
    mem_v = lax.all_to_all(out_v, KEY, split_axis=0, concat_axis=0, tiled=True)

    qmem, qloc, kloc, kraw, v, normed, gains = project(plan, x, cosine, sine, first)
    p_loc, p_mem = weigh(qmem, qloc, kloc, mem_k, local_bias, memory_bias)
    if plan.fast:
        project_out = across_second(after(project_out, p_loc))
        p_mem = after(p_mem, project_out)
        second = project_out + other_core(project_out) + [gate_up]
    attended = attend(p_loc, p_mem, v, mem_v)

    run = tokens // group
    fresh = jnp.stack([kraw.reshape(group, run, width), v.reshape(group, run, width)], axis=1)
    fresh = after(fresh, (p_loc, project_out) if plan.fast else p_loc)
    arrived = lax.all_to_all(fresh, KEY, split_axis=0, concat_axis=0, tiled=True)
    new_keys = jnp.concatenate([cache_keys[:, run:], arrived[:, 0]], axis=1)
    new_values = jnp.concatenate([cache_values[:, run:], arrived[:, 1]], axis=1)

    n_half, ff = plan.halves, gate_proj.shape[1]
    results = feed(plan, x, attended, ct, gains, second, ff)
    g_gu, g_do, (outputs, dmix, datt) = (
        results[0],
        results[1 : 1 + n_half],
        results[1 + n_half :],
    )
    if plan.fast:
        g_gu, g_do = after((g_gu, g_do), arrived)
        g_gu = g_gu.reshape((8,) + g_gu.shape[2:])
        g_gu = lax.psum_scatter(g_gu, ("dp", "core"), scatter_dimension=0, tiled=True)
        g_gu = lax.optimization_barrier(g_gu)
    if plan.fast:
        g_do = both_cores(*g_do)
        datt = after(datt, g_do)
    dq, dk, dv = attend_back(
        p_loc, p_mem, datt, attended, qloc, kloc, v, mem_k, mem_v, cosine, sine
    )
    if plan.fast:
        do_mine, do_passed = over_dp_first(g_do, dq)
        dq = after(dq, do_passed)
    g_qkv = project_grads(plan, normed, dq, dk, dv)
    dq = after(dq, g_qkv)
    if plan.fast:
        do_blocks = over_dp_second(do_mine, do_passed, g_qkv)
        dq = after(dq, do_blocks)
    input_grad = project_back(
        plan, x, dmix, gains, dq, dk, dv, first if plan.fast else first[:1]
    )

    if plan.fast:
        own, swapped = g_qkv[0], swap(g_qkv[1], KEY, 8, 1)
        g_qkv = add(*after((own, swapped), (input_grad, arrived)))
        g_do = over_z(do_blocks, g_qkv)
        g_gu = after(g_gu, g_do)[0]
        mine, passed = over_dp_first(g_qkv, g_gu)
        g_gu = over_z(g_gu, passed)
        blocks = over_dp_second(mine, passed, g_gu)
        g_do = from_dp(g_do, blocks)
        g_qkv = over_z(blocks)
        g_gu = from_dp(g_gu, g_qkv)
        g_qkv = from_dp(g_qkv).astype(F32)
        g_do = g_do.transpose(1, 0, 2).reshape(-1, width).astype(F32)
        total_down, total_out = g_do[:-rows], g_do[-rows:]
        total_gate = g_gu[:, 0].reshape(rows, -1).astype(F32)
        total_up = g_gu[:, 1].reshape(rows, -1).astype(F32)
        each = rows // n_dp
        total_query, total_key, total_value = (
            g_qkv[:, m * each : (m + 1) * each].reshape(rows, width) for m in range(3)
        )
    else:

        def total(g):
            g = lax.psum_scatter(g.astype(F32), KEY, scatter_dimension=0, tiled=True)
            return lax.psum(g.astype(BF16), "dp").astype(F32)

        wide = lambda g: g.transpose(1, 0, 2).reshape(g.shape[1], width)
        total_query, total_key, total_value = (
            total(g_qkv[0][0, 0, m * width : (m + 1) * width]) for m in range(3)
        )
        total_gate, total_up = total(g_gu[0, 0, 0, 0]), total(g_gu[0, 0, 0, 1])
        total_down, total_out = total(wide(g_do[0][:, :ff])), total(wide(g_do[0][:, ff:]))

    def of_gain(gain, *pairs):
        terms = sum(jnp.sum(w.astype(F32) * g, axis=1) for w, g in pairs)
        return terms / gain.astype(F32)

    total_attn = of_gain(
        attn_gain, (query_proj, total_query), (key_proj, total_key), (value_proj, total_value)
    )
    total_ffn = of_gain(ffn_gain, (gate_proj, total_gate), (up_proj, total_up))
    return (
        outputs[None],
        input_grad[None],
        total_query,
        total_key,
        total_value,
        total_out,
        total_gate,
        total_up,
        total_down,
        total_attn,
        total_ffn,
        new_keys,
        new_values,
    )


def solution(mesh):
    n_dp, n_key = mesh.shape["dp"], mesh.shape["key"]
    plan = Plan(n_dp, n_key)
    fine = jax.sharding.Mesh(mesh.devices.reshape(n_dp, n_key // 2, 2), ("dp",) + KEY)
    rows, cache = P(("dp",) + KEY, None, None), P("dp", KEY, None)
    weight, gain = P(KEY, None), P(KEY)
    return jax.shard_map(
        functools.partial(per_device, plan),
        mesh=fine,
        in_specs=(rows, P(("dp",) + KEY, None), P("dp"), P("dp"), cache, cache)
        + (weight,) * 7
        + (gain, gain, rows),
        out_specs=(rows, rows) + (weight,) * 7 + (gain, gain, cache, cache),
        check_vma=False,
    )
```
